1024 devices in a mesh: gx: 8 (over y), gy: 8 (over x), gz: 16 (over z, core).
Axes of the slice: x: 8, y: 8, z: 8, core: 2. Of those that a mesh axis runs over, the one named last changes fastest.
Arguments:
- basis: float32 [27, 64, 64, 2048], P(None, 'gx', 'gy', 'gz'), may hold values from 0.1 to 1
- perm: float32 [3, 64, 64, 2048], P(None, 'gx', 'gy', 'gz'), may hold values from 0.05 to 5
- storage: float32 [64, 64, 2048], P('gx', 'gy', 'gz'), may hold values from 0.05 to 1
- layer: int32 [64, 64, 2048], P('gx', 'gy', 'gz'), may hold values from 0 to 255, as said below
Outputs:
- smoothed_basis: float32 [27, 64, 64, 2048], P(None, 'gx', 'gy', 'gz')
- coarse_operator: float32 [27, 8, 8, 256], P(None, 'gx', 'gy', 'gz')
The draws below stay inside these ranges and needn't reach their ends.
Inputs may be any that keep to these rules, and one draw needn't show every extreme that they name: A cell at vertical index z has layer z // 8 or z // 8 + 1; within a column ids never fall with z, and every layer holds at least one cell of every column.
All inputs are finite; a program needn't handle non-finite values.
Results may differ from the reference program's by a relative error of at most 0.0003.
Values sent between devices are 32-bit elements; how exact they have to be, the bound alone decides.
No kernel may reach another device: no remote copies, remote signals or barrier semaphores. Data moves between devices by JAX's collectives and lax.ppermute only.
A program may use at most 64 MiB of HBM per device.

```python
import math
import jax
import jax.numpy as jnp
from jax import lax

BLOCK = 8
ITERS = 2
NX = 64
NY = 64
NZ = 2048
NBX = 8
NBY = 8
NL = 256


def draw_layer(key, part):
    key = jax.random.fold_in(key, 11)
    tops = jax.random.randint(key, (NX, NY, NL), 0, BLOCK, dtype=jnp.int32)
    following = jnp.concatenate([tops[:, :, 1:], jnp.zeros((NX, NY, 1), jnp.int32)], axis=2)
    per_cell = jnp.repeat(following, BLOCK, axis=2)
    depth = jnp.arange(NZ, dtype=jnp.int32)
    lifted = ((depth % BLOCK)[None, None, :] >= BLOCK - per_cell).astype(jnp.int32)
    return (depth // BLOCK)[None, None, :] + lifted


def block_scale(own_key, shape, shards, least, high):
    loudness = 1.0
    for axis_at, blocks in shards:
        draws = jax.random.uniform(jax.random.fold_in(jax.random.fold_in(own_key, 6), axis_at), (blocks,), jnp.float32, least / len(shards), high / len(shards))
        loudness = loudness * jnp.repeat(jnp.exp(draws), shape[axis_at] // blocks).reshape((-1,) + (1,) * (len(shape) - 1 - axis_at))
    return loudness


def setup_inputs(seed: int = 0) -> dict:
    key_of = jax.random.split(jax.random.key(seed), 5)
    return {
        "basis": jnp.clip(jnp.exp(math.log(1.0) - 2.3025851 * jax.random.uniform(key_of[0], (27, NX, NY, NZ), jnp.float32) ** block_scale(key_of[0], (27, NX, NY, NZ), ((1, 8), (2, 8), (3, 16)), -0.2, 0.2)), 0.1, 1.0),
        "perm": jnp.clip(jnp.exp(math.log(5.0) - 4.6051702 * jax.random.uniform(key_of[1], (3, NX, NY, NZ), jnp.float32) ** block_scale(key_of[1], (3, NX, NY, NZ), ((1, 8), (2, 8), (3, 16)), -0.2, 0.2)), 0.05, 5.0),
        "storage": jnp.clip(jnp.exp(math.log(1.0) - 2.9957323 * jax.random.uniform(key_of[2], (NX, NY, NZ), jnp.float32) ** block_scale(key_of[2], (NX, NY, NZ), ((0, 8), (1, 8), (2, 16)), -0.2, 0.2)), 0.05, 1.0),
        "layer": draw_layer(jax.random.fold_in(key_of[4], 71), 0),
    }


relax_weight = 2.0 / 3.0


def harmonic(first, second):
    total = first + second
    return 2.0 * first * second / jnp.where(total > 0.0, total, 1.0)


def apply_operator(values, perm_pad, storage_pad):
    perm_x = perm_pad[0]
    perm_y = perm_pad[1]
    perm_z = perm_pad[2]
    face_x = harmonic(perm_x[:-1, 1:-1, 1:-1], perm_x[1:, 1:-1, 1:-1])
    face_y = harmonic(perm_y[1:-1, :-1, 1:-1], perm_y[1:-1, 1:, 1:-1])
    face_z = harmonic(perm_z[1:-1, 1:-1, :-1], perm_z[1:-1, 1:-1, 1:])
    diagonal = storage_pad[1:-1, 1:-1, 1:-1] + face_x[:-1] + face_x[1:]
    diagonal = diagonal + face_y[:, :-1] + face_y[:, 1:] + face_z[:, :, :-1] + face_z[:, :, 1:]
    beside = face_x[:-1] * values[..., :-2, 1:-1, 1:-1] + face_x[1:] * values[..., 2:, 1:-1, 1:-1]
    beside = beside + face_y[:, :-1] * values[..., 1:-1, :-2, 1:-1] + face_y[:, 1:] * values[..., 1:-1, 2:, 1:-1]
    beside = beside + face_z[:, :, :-1] * values[..., 1:-1, 1:-1, :-2] + face_z[:, :, 1:] * values[..., 1:-1, 1:-1, 2:]
    return diagonal * values[..., 1:-1, 1:-1, 1:-1] - beside, diagonal


def lateral_cover(coords, total, blocks):
    lower = (coords + BLOCK // 2) // BLOCK - 1
    upper = lower + 1
    residue = jnp.arange(3, dtype=jnp.int32)[:, None]
    inside = (coords >= 0) & (coords < total)
    hit = ((lower >= 0) & (lower % 3 == residue)) | ((upper < blocks) & (upper % 3 == residue))
    return (hit & inside[None, :]).astype(jnp.float32)


def reference(basis, perm, storage, layer):
    coord_x = jnp.arange(NX, dtype=jnp.int32)
    coord_y = jnp.arange(NY, dtype=jnp.int32)
    cover_x = lateral_cover(coord_x, NX, NBX)
    cover_y = lateral_cover(coord_y, NY, NBY)
    residue_z = layer % 3
    perm_pad = jnp.pad(perm, ((0, 0), (1, 1), (1, 1), (1, 1)))
    storage_pad = jnp.pad(storage, 1)
    slots = jnp.arange(27, dtype=jnp.int32)
    widths = ((0, 0), (1, 1), (1, 1), (1, 1))

    def slot_support(slot):
        vertical = (residue_z == slot // 9).astype(jnp.float32)
        return vertical * cover_y[(slot // 3) % 3][None, :, None] * cover_x[slot % 3][:, None, None]

    def start(pair):
        return slot_support(pair[0]) * pair[1]

    def relax(pair):
        image, diagonal = apply_operator(pair[1], perm_pad, storage_pad)
        centre = pair[1][1:-1, 1:-1, 1:-1]
        return centre - relax_weight * slot_support(pair[0]) * image / jnp.where(diagonal > 0.0, diagonal, 1.0)

    values = lax.map(start, (slots, basis))
    for sweep in range(ITERS):
        updated = lax.map(relax, (slots, jnp.pad(values, widths)))
        total = jnp.sum(updated, axis=0)
        values = updated / jnp.where(total > 0.0, total, 1.0)

    depth = jnp.arange(NZ, dtype=jnp.int32)
    lifted = (layer - depth[None, None, :] // BLOCK).astype(jnp.float32)

    def assemble(slab):
        image, diagonal = apply_operator(slab, perm_pad, storage_pad)
        lower = (image * (1.0 - lifted)).reshape(NBX, BLOCK, NBY, BLOCK, NL, BLOCK).sum(axis=(1, 3, 5))
        upper = (image * lifted).reshape(NBX, BLOCK, NBY, BLOCK, NL, BLOCK).sum(axis=(1, 3, 5))
        return lower + jnp.pad(upper, ((0, 0), (0, 0), (1, 0)))[:, :, :NL]

    partial_value = lax.map(assemble, jnp.pad(values, widths))
    offsets = jnp.arange(27, dtype=jnp.int32)[:, None, None, None]
    block_x = jnp.arange(NBX, dtype=jnp.int32)[None, :, None, None]
    block_y = jnp.arange(NBY, dtype=jnp.int32)[None, None, :, None]
    rows = jnp.arange(NL, dtype=jnp.int32)[None, None, None, :]
    choose = 9 * ((rows + offsets // 9 - 1) % 3) + 3 * ((block_y + (offsets // 3) % 3 - 1) % 3) + (block_x + offsets % 3 - 1) % 3
    choose = jnp.broadcast_to(choose, (27, NBX, NBY, NL)).astype(jnp.int32)
    coarse = jnp.take_along_axis(partial_value, choose, axis=0) * (1.0 / (BLOCK * BLOCK))
    return values, coarse
```

```python
import jax
import jax.numpy as jnp
from jax import lax
from jax.experimental import pallas as pl
from jax.experimental.pallas import tpu as pltpu
from jax.sharding import PartitionSpec as P

BLOCK = 8
FIELDS = 9
PX, PY, PZ, STORAGE, LAYER = 4, 5, 6, 7, 8
ALL = tuple(range(FIELDS))
FIELDS_X = (ALL, ALL, (0, 1, 2, 3, PX, LAYER))
FIELDS_Y = (ALL, ALL, (0, 1, 2, 3, PY, LAYER))
ROWS_Y = 8 * sum(len(f) for f in FIELDS_Y)
ROWS_X = 8 * sum(len(f) for f in FIELDS_X)
F32 = jnp.float32


def iota(shape, dim):
    return lax.broadcasted_iota(jnp.int32, shape, dim)


def roll(value, shift, axis):
    return pltpu.roll(value, shift % value.shape[axis], axis)


def pack_kernel(basis, perm, storage, layer, core, edge):
    gx, gy = lax.axis_index("gx"), lax.axis_index("gy")
    nx, ny = lax.axis_size("gx"), lax.axis_size("gy")
    sub, lane = iota((8, 128), 0), iota((8, 128), 1)
    ids = layer[...].astype(F32)
    residue = ids - 3.0 * jnp.floor((ids + 0.5) * (1.0 / 3.0))
    is_zero, is_one = residue < 0.5, residue < 1.5
    rx_own, rx_low, rx_high = gx % 3, (gx + 2) % 3, (gx + 1) % 3
    ry_own, ry_low, ry_high = gy % 3, (gy + 2) % 3, (gy + 1) % 3
    low_rows = sub < 4
    y_valid = jnp.where(low_rows, (gy > 0).astype(F32), (gy < ny - 1).astype(F32))

    def at(rx, ry, x):
        first, second, third = (basis[9 * rz + 3 * ry + rx, x] for rz in range(3))
        return jnp.where(is_zero[x], first, jnp.where(is_one[x], second, third))

    for x in range(8):
        rx_other = rx_low if x < 4 else rx_high
        x_valid = ((gx > 0) if x < 4 else (gx < nx - 1)).astype(F32)
        for ex, rx in enumerate((rx_own, rx_other)):
            own = at(rx, ry_own, x)
            other = jnp.where(low_rows, at(rx, ry_low, x), at(rx, ry_high, x)) * y_valid
            if ex:
                own, other = own * x_valid, other * x_valid
            core[2 * ex, 8 * x : 8 * x + 8] = own
            core[2 * ex + 1, 8 * x : 8 * x + 8] = other
        for d in range(3):
            core[PX + d, 8 * x : 8 * x + 8] = perm[d, x]
        core[STORAGE, 8 * x : 8 * x + 8] = storage[x]
        core[LAYER, 8 * x : 8 * x + 8] = ids[x]
    for f in ALL:
        packed = jnp.zeros((8, 128), F32)
        for x in range(8):
            value = core[f, 8 * x : 8 * x + 8]
            value = jnp.where(lane < 4, value, roll(value, 16, 1))
            packed = jnp.where(lane // 16 == x, roll(value, 16 * x, 1), packed)
        edge[f] = packed


def y_kernel(core, from_low, from_high, beside_z, to_low, to_high):
    lane = iota((8, 128), 1)
    for f in ALL:
        beside_z[f] = jnp.where(lane % 16 < 4, from_high[f], from_low[f])
    for out, side in ((to_low, 0), (to_high, 1)):
        at = 0
        for d, fields in enumerate(FIELDS_Y):
            y = 7 - d if side else d
            for f in fields:
                out[at : at + 8] = core[f, pl.ds(y, 8, stride=8), :]
                at += 8
        for d in range(3):
            y = 7 - d if side else d
            for f in ALL:
                out[at : at + 1] = beside_z[f, y : y + 1]
                at += 1


def x_kernel(core, beside_z, from_low, from_high, beside_y, corner, to_low, to_high):
    sub, lane = iota((8, 128), 0), iota((8, 128), 1)
    beside_y[...] = jnp.zeros(beside_y.shape, F32)
    corner[...] = jnp.zeros(corner.shape, F32)
    for source, side in ((from_low, 0), (from_high, 1)):
        at = 0
        for d, fields in enumerate(FIELDS_Y):
            row = d if side else 7 - d
            for f in fields:
                into = f ^ 1 if f < 4 else f
                beside_y[into, pl.ds(row, 8, stride=8), :] = source[at : at + 8]
                at += 8
        for d in range(3):
            row = d if side else 7 - d
            for f in ALL:
                into = f ^ 1 if f < 4 else f
                corner[into, row : row + 1] = source[at : at + 1]
                at += 1
    for out, side in ((to_low, 0), (to_high, 1)):
        at = 0
        for d, fields in enumerate(FIELDS_X):
            x = 7 - d if side else d
            for f in fields:
                out[at : at + 8] = core[f, 8 * x : 8 * x + 8]
                at += 8
        first, second = (7, 6) if side else (0, 1)
        for f in ALL:
            out[at : at + 8] = jnp.where(
                (sub == 2) | (sub == 3),
                roll(beside_y[f, 8 * second : 8 * second + 8], 3, 0),
                beside_y[f, 8 * first : 8 * first + 8],
            )
            at += 8
        for f in ALL:
            out[at : at + 8] = jnp.where(
                (lane >= 48) & (lane < 80), roll(corner[f], -48 if side else 48, 1), beside_z[f]
            )
            at += 8


def harmonic(first, second):
    total = first + second
    return 2.0 * first * second / jnp.where(total > 0.0, total, 1.0)


def sweep_kernel(
    core, beside_z, beside_y, corner, from_low, from_high, smoothed, coarse,
    ext, face_x, face_y, face_z, near_x, near_y, near_y_other, near_z, diagonal, weight, once, twice, sums,
):
    gx, gy, gz = lax.axis_index("gx"), lax.axis_index("gy"), lax.axis_index("gz")
    nx, ny = lax.axis_size("gx"), lax.axis_size("gy")
    sub, lane = iota((8, 128), 0), iota((8, 128), 1)
    row = iota((16, 256), 0)
    column = iota((16, 256), 1)

    def unpacked(value, slot):
        value = roll(value, -16 * slot, 1)
        return jnp.where(lane < 3, value, jnp.where(lane >= 117, roll(value, 112, 1), 0.0))

    zero = jnp.zeros((8, 128), F32)
    for f in ALL:
        for x in range(8):
            ext[f, x + 3, 0:8, 0:128] = core[f, 8 * x : 8 * x + 8]
            ext[f, x + 3, 8:16, 0:128] = beside_y[f, 8 * x : 8 * x + 8]
            ext[f, x + 3, 0:8, 128:256] = unpacked(beside_z[f], x)
            ext[f, x + 3, 8:16, 128:256] = unpacked(corner[f], x)
    for source, side in ((from_low, 0), (from_high, 1)):
        at = 0
        for d in range(3):
            plane = 11 + d if side else 2 - d
            for f in ALL:
                into = f ^ 2 if f < 4 else f
                if f in FIELDS_X[d]:
                    ext[into, plane, 0:8, 0:128] = source[at : at + 8]
                    at += 8
                else:
                    ext[into, plane, 0:8, 0:128] = zero
        for f in ALL:
            into = f ^ 2 if f < 4 else f
            rows = source[at : at + 8]
            across = source[at + 72 : at + 80]
            at += 8
            lateral = roll(across, -48 if side else 48, 1)
            for d in range(3):
                plane = 11 + d if side else 2 - d
                slot = d if side else 7 - d
                ext[into, plane, 0:8, 128:256] = unpacked(across, slot)
                if d == 0:
                    ext[into, plane, 8:16, 0:128] = jnp.where((sub < 2) | (sub > 5), rows, 0.0)
                elif d == 1:
                    ext[into, plane, 8:16, 0:128] = jnp.where((sub < 1) | (sub > 6), roll(rows, -3, 0), 0.0)
                else:
                    ext[into, plane, 8:16, 0:128] = zero
                ext[into, plane, 8:16, 128:256] = unpacked(lateral, slot) if d < 2 else zero

    for p in range(13):
        face = harmonic(ext[PX, p], ext[PX, p + 1])
        face_x[p] = face
        near_x[p] = jnp.where(ext[LAYER, p] == ext[LAYER, p + 1], face, 0.0)
    for p in range(1, 13):
        ids = ext[LAYER, p]
        across = ext[PY, p]
        face = harmonic(across, roll(across, -1, 0))
        face_y[p] = face
        near = jnp.where(ids == roll(ids, -1, 0), face, 0.0)
        near_y[p] = near
        near_y_other[p] = jnp.where(row == 3, 0.0, near)
        total = ext[STORAGE, p] + face_x[p - 1] + face_x[p] + face + roll(face, 1, 0)
        across = ext[PZ, p]
        face = harmonic(across, roll(across, -1, 1))
        face_z[p] = face
        near_z[p] = jnp.where(ids == roll(ids, -1, 1), face, 0.0)
        total = total + face + roll(face, 1, 1)
        diagonal[p] = total
        weight[p] = (2.0 / 3.0) / jnp.where(total > 0.0, total, 1.0)

    y_valid = jnp.where((row < 4) | (row >= 12), (gy > 0).astype(F32), (gy < ny - 1).astype(F32))

    def relax(values, p):
        x_valid = ((gx > 0) if p < 7 else (gx < nx - 1)).astype(F32)
        updated = []
        for f in range(4):
            own = values(f, p)
            side_y = near_y_other[p] if f & 1 else near_y[p]
            total = side_y * roll(own, -1, 0) + roll(side_y * own, 1, 0)
            side_z = near_z[p]
            total = total + side_z * roll(own, -1, 1) + roll(side_z * own, 1, 1)
            if not (f & 2 and p == 7):
                total = total + near_x[p - 1] * values(f, p - 1)
            if not (f & 2 and p == 6):
                total = total + near_x[p] * values(f, p + 1)
            scale = weight[p]
            if f & 1:
                scale = scale * y_valid
            if f & 2:
                scale = scale * x_valid
            updated.append(own * (1.0 / 3.0) + scale * total)
        total = (updated[0] + updated[1]) + (updated[2] + updated[3])
        inverse = 1.0 / jnp.where(total > 0.0, total, 1.0)
        return [value * inverse for value in updated]

    for p in range(1, 13):
        for f, value in enumerate(relax(lambda f, p: ext[f, p], p)):
            once[f, p] = value
    for p in range(2, 12):
        for f, value in enumerate(relax(lambda f, p: once[f, p], p)):
            twice[f, p] = value

    rx_own, rx_low, rx_high = gx % 3, (gx + 2) % 3, (gx + 1) % 3
    ry_own, ry_low, ry_high = gy % 3, (gy + 2) % 3, (gy + 1) % 3
    for x in range(8):
        ids = ext[LAYER, x + 3, 0:8, 0:128]
        residue = ids - 3.0 * jnp.floor((ids + 0.5) * (1.0 / 3.0))
        rx_other, rx_none = (rx_low, rx_high) if x < 4 else (rx_high, rx_low)
        for rz in range(3):
            hit = jnp.abs(residue - rz) < 0.5
            for ex, rx in ((0, rx_own), (1, rx_other)):
                own = jnp.where(hit, twice[2 * ex, x + 3, 0:8, 0:128], 0.0)
                other = jnp.where(hit, twice[2 * ex + 1, x + 3, 0:8, 0:128], 0.0)
                smoothed[9 * rz + 3 * ry_own + rx, x] = own
                smoothed[9 * rz + 3 * ry_low + rx, x] = jnp.where(sub < 4, other, 0.0)
                smoothed[9 * rz + 3 * ry_high + rx, x] = jnp.where(sub < 4, 0.0, other)
            for ry in range(3):
                smoothed[9 * rz + 3 * ry + rx_none, x] = zero

    first_octet = gz * (128 // BLOCK)
    octet = (jnp.where(column < 192, column, column - 256) + 256) // BLOCK - 32 + first_octet
    octet = octet.astype(F32)
    sums[...] = jnp.zeros(sums.shape, F32)
    for p in range(2, 12):
        inside = 3 <= p <= 10
        tall = 16 if inside else 8
        ids = ext[LAYER, p, 0:tall]
        lifted = ids > octet[0:tall]
        parts = [jnp.zeros((tall, 256), F32) for _ in range(3)]

        def add(parts, face, step, keep=None):
            if keep is not None:
                face = jnp.where(keep, face, 0.0)
            return [
                parts[0] - jnp.where(step == 1.0, face, 0.0),
                parts[1] - jnp.where(step == 0.0, face, 0.0),
                parts[2] - jnp.where(step == -1.0, face, 0.0),
            ]

        in_block = row[0:tall] < 8
        if p >= 4:
            parts = add(parts, face_x[p - 1, 0:tall], ext[LAYER, p - 1, 0:tall] - ids, in_block)
        if p <= 9:
            parts = add(parts, face_x[p, 0:tall], ext[LAYER, p + 1, 0:tall] - ids, in_block)
        if inside:
            face = face_y[p]
            parts = add(parts, face, roll(ids, -1, 0) - ids, (row < 7) | (row == 15))
            parts = add(parts, roll(face, 1, 0), roll(ids, 1, 0) - ids, (row > 0) & (row < 9))
            face = face_z[p]
            parts = add(parts, face, roll(ids, -1, 1) - ids, in_block)
            parts = add(parts, roll(face, 1, 1), roll(ids, 1, 1) - ids, in_block)
            parts[1] = parts[1] + jnp.where(in_block, diagonal[p], 0.0)
        for oz in range(3):
            upper = jnp.where(lifted, parts[oz], 0.0)
            lower = parts[oz] - upper
            for f in range(4):
                value = twice[f, p, 0:tall]
                ox = 1 if f < 2 else (0 if p < 7 else 2)
                sums[oz, 0, ox, f & 1, 0:tall] += lower * value
                sums[oz, 1, ox, f & 1, 0:tall] += upper * value
    spot = iota((256, 128), 0)
    place = (jnp.where(spot < 192, spot, spot - 256) + 256) // BLOCK - 32
    for oz in range(3):
        total = jnp.zeros((16, 128), F32)
        for lift in range(2):
            rows = []
            for oy in range(3):
                for ox in range(3):
                    if oy == 1:
                        value = sums[oz, lift, ox, 0]
                        value = value[0:8] + value[8:16]
                    else:
                        value = sums[oz, lift, ox, 1]
                        value = value[0:8] + roll(value[8:16], 4, 0)
                        value = value[0:4] if oy == 0 else value[4:8]
                    rows.append(jnp.sum(value, axis=0, keepdims=True))
            rows.append(jnp.zeros((7, 256), F32))
            chosen = (place + lift - (oz - 1) == iota((256, 128), 1)).astype(F32)
            total = total + jnp.dot(
                jnp.concatenate(rows, axis=0), chosen, precision=lax.Precision.HIGHEST, preferred_element_type=F32
            )
        total = total * (1.0 / (BLOCK * BLOCK))
        coarse[9 * oz : 9 * oz + 9] = total[0:9, 0:16]


def call(kernel, shapes, *operands, scratch=()):
    vmem = pl.BlockSpec(memory_space=pltpu.VMEM)
    return pl.pallas_call(
        kernel,
        out_shape=[jax.ShapeDtypeStruct(shape, F32) for shape in shapes],
        in_specs=[vmem] * len(operands),
        out_specs=[vmem] * len(shapes),
        scratch_shapes=[pltpu.VMEM(shape, F32) for shape in scratch],
        compiler_params=pltpu.CompilerParams(vmem_limit_bytes=48 * 1024 * 1024),
    )(*operands)


def exchange(axis, to_low, to_high):
    count = lax.axis_size(axis)
    forward = [(i, i + 1) for i in range(count - 1)]
    backward = [(target, source) for source, target in forward]
    return lax.ppermute(to_high, axis, forward), lax.ppermute(to_low, axis, backward)


def per_device(basis, perm, storage, layer):
    block = (FIELDS, 64, 128)
    side = (FIELDS, 8, 128)
    core, edge = call(pack_kernel, (block, side), basis, perm, storage, layer)
    low, high = exchange("gz", edge, edge)
    rows = (ROWS_Y + 32, 128)
    beside_z, to_low, to_high = call(y_kernel, (side, rows, rows), core, low, high)
    low, high = exchange("gy", to_low, to_high)
    rows = (ROWS_X + 144, 128)
    beside_y, corner, to_low, to_high = call(x_kernel, (block, side, rows, rows), core, beside_z, low, high)
    low, high = exchange("gx", to_low, to_high)
    field = (14, 16, 256)
    smoothed, coarse = call(
        sweep_kernel,
        ((27, 8, 8, 128), (27, 16)),
        core,
        beside_z,
        beside_y,
        corner,
        low,
        high,
        scratch=((FIELDS,) + field,) + (field,) * 9 + ((4,) + field,) * 2 + ((3, 2, 3, 2, 16, 256),),
    )
    return smoothed, coarse.reshape(27, 1, 1, 16)


def solution(mesh):
    return jax.shard_map(
        per_device,
        mesh=mesh,
        in_specs=(
            P(None, "gx", "gy", "gz"),
            P(None, "gx", "gy", "gz"),
            P("gx", "gy", "gz"),
            P("gx", "gy", "gz"),
        ),
        out_specs=(P(None, "gx", "gy", "gz"), P(None, "gx", "gy", "gz")),
        check_vma=False,
    )
```

```python
import jax
import jax.numpy as jnp
from jax import lax
from jax.experimental import pallas as pl
from jax.experimental.pallas import tpu as pltpu
from jax.sharding import PartitionSpec as P

BLOCK = 8
FIELDS = 9
PX, PY, PZ, STORAGE, LAYER = 4, 5, 6, 7, 8
ALL = tuple(range(FIELDS))
FIELDS_X = (ALL, ALL, (0, 1, 2, 3, PX, LAYER))
FIELDS_Y = (ALL, ALL, (0, 1, 2, 3, PY, LAYER))
ROWS_Y = 8 * sum(len(f) for f in FIELDS_Y)
ROWS_X = 8 * sum(len(f) for f in FIELDS_X)
F32 = jnp.float32


def iota(shape, dim):
    return lax.broadcasted_iota(jnp.int32, shape, dim)


def roll(value, shift, axis):
    return pltpu.roll(value, shift % value.shape[axis], axis)


def pack_kernel(basis_hbm, perm_hbm, storage_hbm, layer_hbm, core, edge, basis, layer, sems):
    copies = [
        pltpu.make_async_copy(source, target, sems.at[i])
        for i, (source, target) in enumerate(
            (
                (basis_hbm, basis),
                (layer_hbm, layer),
                (perm_hbm, core.at[PX : PZ + 1]),
                (storage_hbm, core.at[STORAGE]),
            )
        )
    ]
    for copy in copies:
        copy.start()
    gx, gy = lax.axis_index("gx"), lax.axis_index("gy")
    nx, ny = lax.axis_size("gx"), lax.axis_size("gy")
    sub, lane = iota((8, 128), 0), iota((8, 128), 1)
    rx_own, rx_low, rx_high = gx % 3, (gx + 2) % 3, (gx + 1) % 3
    ry_own, ry_low, ry_high = gy % 3, (gy + 2) % 3, (gy + 1) % 3
    low_rows = sub < 4
    y_valid = jnp.where(low_rows, (gy > 0).astype(F32), (gy < ny - 1).astype(F32))
    for copy in copies:
        copy.wait()
    ids = layer[...].astype(F32)
    core[LAYER] = ids
    residue = ids - 3.0 * jnp.floor((ids + 0.5) * (1.0 / 3.0))

    for x in range(8):
        here = residue[8 * x : 8 * x + 8]
        is_zero, is_one = here < 0.5, here < 1.5

        def at(rx, ry):
            first, second, third = (basis[9 * rz + 3 * ry + rx, 8 * x : 8 * x + 8] for rz in range(3))
            return jnp.where(is_zero, first, jnp.where(is_one, second, third))

        rx_other = rx_low if x < 4 else rx_high
        x_valid = ((gx > 0) if x < 4 else (gx < nx - 1)).astype(F32)
        for ex, rx in enumerate((rx_own, rx_other)):
            own = at(rx, ry_own)
            other = jnp.where(low_rows, at(rx, ry_low), at(rx, ry_high)) * y_valid
            if ex:
                own, other = own * x_valid, other * x_valid
            core[2 * ex, 8 * x : 8 * x + 8] = own
            core[2 * ex + 1, 8 * x : 8 * x + 8] = other
    for f in ALL:
        packed = jnp.zeros((8, 128), F32)
        for x in range(8):
            value = core[f, 8 * x : 8 * x + 8]
            value = jnp.where(lane < 4, value, roll(value, 16, 1))
            packed = jnp.where(lane // 16 == x, roll(value, 16 * x, 1), packed)
        edge[f] = packed


def by_side(axis, one, other, body):
    even = lax.axis_index(axis) % 2 == 0
    pl.when(even)(lambda: body(((one, 1), (other, 0))))
    pl.when(jnp.logical_not(even))(lambda: body(((one, 0), (other, 1))))


def y_kernel(core, from_one, from_other, beside_z, to_one, to_other):
    lane = iota((8, 128), 1)
    high = (lane % 16 < 4).astype(jnp.int32)
    odd = lax.axis_index("gz") % 2
    for f in ALL:
        beside_z[f] = jnp.where(high != odd, from_one[f], from_other[f])

    def send(pairs):
        for out, side in pairs:
            at = 0
            for d, fields in enumerate(FIELDS_Y):
                y = 7 - d if side else d
                for f in fields:
                    out[at : at + 8] = core[f, pl.ds(y, 8, stride=8), :]
                    at += 8
            for d in range(3):
                y = 7 - d if side else d
                for f in ALL:
                    out[at : at + 1] = beside_z[f, y : y + 1]
                    at += 1

    by_side("gy", to_one, to_other, send)


def x_kernel(core, beside_z, from_one, from_other, beside_y, corner, to_one, to_other):
    sub, lane = iota((8, 128), 0), iota((8, 128), 1)
    beside_y[...] = jnp.zeros(beside_y.shape, F32)
    corner[...] = jnp.zeros(corner.shape, F32)

    def receive(pairs):
        for source, side in pairs:
            at = 0
            for d, fields in enumerate(FIELDS_Y):
                row = d if side else 7 - d
                for f in fields:
                    into = f ^ 1 if f < 4 else f
                    beside_y[into, pl.ds(row, 8, stride=8), :] = source[at : at + 8]
                    at += 8
            for d in range(3):
                row = d if side else 7 - d
                for f in ALL:
                    into = f ^ 1 if f < 4 else f
                    corner[into, row : row + 1] = source[at : at + 1]
                    at += 1

    by_side("gy", from_one, from_other, receive)

    def send(pairs):
        for out, side in pairs:
            at = 0
            for d, fields in enumerate(FIELDS_X):
                x = 7 - d if side else d
                for f in fields:
                    out[at : at + 8] = core[f, 8 * x : 8 * x + 8]
                    at += 8
            first, second = (7, 6) if side else (0, 1)
            for f in ALL:
                out[at : at + 8] = jnp.where(
                    (sub == 2) | (sub == 3),
                    roll(beside_y[f, 8 * second : 8 * second + 8], 3, 0),
                    beside_y[f, 8 * first : 8 * first + 8],
                )
                at += 8
            for f in ALL:
                out[at : at + 8] = jnp.where(
                    (lane >= 48) & (lane < 80), roll(corner[f], -48 if side else 48, 1), beside_z[f]
                )
                at += 8

    by_side("gx", to_one, to_other, send)


def harmonic(first, second):
    total = first + second
    return 2.0 * first * second / jnp.where(total > 0.0, total, 1.0)


def unpacked(value, slot):
    lane = iota((8, 128), 1)
    value = roll(value, -16 * slot, 1)
    return jnp.where(lane < 3, value, jnp.where(lane >= 117, roll(value, 112, 1), 0.0))


class Planes:
    def __init__(self, inner, outer, first):
        self.inner, self.outer, self.first, self.last = inner, outer, first, 13 - first

    def at(self, p, shift=0):
        if self.first <= p <= self.last - shift:
            return self.inner, p - self.first
        return self.outer, p


def read(planes, p, f=None, tall=16, shift=0):
    ref, p = planes.at(p, shift)
    return ref[p, 0:tall] if f is None else ref[f, p, 0:tall]


def write(planes, value, p, f=None, shift=0):
    ref, p = planes.at(p, shift)
    rows = value.shape[0]
    if f is None:
        ref[p, 0:rows] = value
    else:
        ref[f, p, 0:rows] = value


class Block:
    def __init__(self, inner, outer):
        names = ("ext", "face_x", "near_x", "face_y", "face_z", "near_y", "near_z", "rest", "weight", "once", "twice")
        first = (3, 3, 3, 3, 3, 3, 3, 3, 4, 4, 5)
        for i, name in enumerate(names):
            setattr(self, name, Planes(inner[i], outer[i] if outer else None, first[i]))
        self.row, self.column = iota((16, 256), 0), iota((16, 256), 1)

    def cells(self, f, p, tall=16):
        return read(self.ext, p, f, tall)

    def side_x(self, planes, p, tall=16):
        return read(planes, p, None, tall, 1)

    def faces_x(self, planes):
        for p in planes:
            face = harmonic(self.cells(PX, p), self.cells(PX, p + 1))
            write(self.face_x, face, p, None, 1)
            write(self.near_x, jnp.where(self.cells(LAYER, p) == self.cells(LAYER, p + 1), face, 0.0), p, None, 1)

    def faces(self, planes):
        for p in planes:
            ids = self.cells(LAYER, p)
            total = self.cells(STORAGE, p)
            for f, axis, face_at, near_at in ((PY, 0, self.face_y, self.near_y), (PZ, 1, self.face_z, self.near_z)):
                across = self.cells(f, p)
                face = harmonic(across, roll(across, -1, axis))
                write(face_at, face, p)
                write(near_at, jnp.where(ids == roll(ids, -1, axis), face, 0.0), p)
                total = total + (face + roll(face, 1, axis))
            write(self.rest, total, p)

    def diagonal(self, p):
        return read(self.rest, p) + (self.side_x(self.face_x, p - 1) + self.side_x(self.face_x, p))

    def weights(self, planes):
        for p in planes:
            total = self.diagonal(p)
            write(self.weight, (2.0 / 3.0) / jnp.where(total > 0.0, total, 1.0), p)

    def relax(self, planes, source, target):
        gx, gy = lax.axis_index("gx"), lax.axis_index("gy")
        nx, ny = lax.axis_size("gx"), lax.axis_size("gy")
        row = self.row
        y_valid = jnp.where((row < 4) | (row >= 12), (gy > 0).astype(F32), (gy < ny - 1).astype(F32))
        for p in planes:
            tall = 8 if (source is self.ext and p in (1, 12)) or (source is self.once and p in (2, 11)) else 16
            x_valid = ((gx > 0) if p < 7 else (gx < nx - 1)).astype(F32)
            near_y, near_z = read(self.near_y, p), read(self.near_z, p, None, tall)
            near_y_other = jnp.where(row == 3, 0.0, near_y)
            low, high = self.side_x(self.near_x, p - 1, tall), self.side_x(self.near_x, p, tall)
            scale = read(self.weight, p, None, tall)
            scale_other = scale * y_valid[0:tall]
            updated = []
            for f in range(4):
                whole = read(source, p, f)
                own = whole[0:tall]
                side = near_y_other if f & 1 else near_y
                total = side[0:tall] * roll(whole, -1, 0)[0:tall] + roll(side * whole, 1, 0)[0:tall]
                total = total + (near_z * roll(own, -1, 1) + roll(near_z * own, 1, 1))
                if not (f & 2 and p == 7):
                    total = total + low * read(source, p - 1, f, tall)
                if not (f & 2 and p == 6):
                    total = total + high * read(source, p + 1, f, tall)
                factor = scale_other if f & 1 else scale
                if f & 2:
                    factor = factor * x_valid
                updated.append(own * (1.0 / 3.0) + factor * total)
            total = (updated[0] + updated[1]) + (updated[2] + updated[3])
            inverse = 1.0 / jnp.where(total > 0.0, total, 1.0)
            for f in range(4):
                write(target, updated[f] * inverse, p, f)

    def coarse_parts(self, planes, parts):
        row, column = self.row, self.column
        octet = (jnp.where(column < 192, column, column - 256) + 256) // BLOCK - 32
        octet = (octet + lax.axis_index("gz") * (128 // BLOCK)).astype(F32)
        in_block = row < 8
        for p in planes:
            inside = 3 <= p <= 10
            tall = 16 if inside else 8
            ids = self.cells(LAYER, p, tall)
            lifted = ids > octet[0:tall]
            keep = in_block[0:tall]
            given = []
            if p >= 4:
                given.append((self.side_x(self.face_x, p - 1, tall), self.cells(LAYER, p - 1, tall), keep))
            if p <= 9:
                given.append((self.side_x(self.face_x, p, tall), self.cells(LAYER, p + 1, tall), keep))
            total = [jnp.zeros((tall, 256), F32) for _ in range(3)]
            if inside:
                face = read(self.face_y, p)
                given.append((face, roll(ids, -1, 0), (row < 7) | (row == 15)))
                given.append((roll(face, 1, 0), roll(ids, 1, 0), (row > 0) & (row < 9)))
                face = read(self.face_z, p)
                given.append((face, roll(ids, -1, 1), keep))
                given.append((roll(face, 1, 1), roll(ids, 1, 1), keep))
                total[1] = jnp.where(keep, self.diagonal(p), 0.0)
            for face, beside, kept in given:
                face = jnp.where(kept, face, 0.0)
                step = beside - ids
                total[0] = total[0] - jnp.where(step == 1.0, face, 0.0)
                total[1] = total[1] - jnp.where(step == 0.0, face, 0.0)
                total[2] = total[2] - jnp.where(step == -1.0, face, 0.0)
            for oz in range(3):
                upper = jnp.where(lifted, total[oz], 0.0)
                parts[oz, 0, p, 0:tall] = total[oz] - upper
                parts[oz, 1, p, 0:tall] = upper

    def coarse_sums(self, planes, parts, sums):
        for oz in range(3):
            for lift in range(2):
                for f in range(4):
                    groups = (planes,) if f < 2 else ([p for p in planes if p < 7], [p for p in planes if p >= 7])
                    for i, group in enumerate(groups):
                        top = bottom = None
                        for p in group:
                            value = parts[oz, lift, p, 0:8] * read(self.twice, p, f, 8)
                            top = value if top is None else top + value
                            if 3 <= p <= 10:
                                ref, at = self.twice.at(p)
                                value = parts[oz, lift, p, 8:16] * ref[f, at, 8:16]
                                bottom = value if bottom is None else bottom + value
                        ox = 1 if f < 2 else 2 * i
                        sums[oz, lift, ox, f & 1] = top + (roll(bottom, 4, 0) if f & 1 else bottom)


def inner_kernel(core, beside_z, beside_y, corner, *refs):
    arrays, parts, sums = refs[:11], refs[12], refs[11]
    ext = arrays[0]
    for f in ALL:
        for x in range(8):
            ext[f, x, 0:8, 0:128] = core[f, 8 * x : 8 * x + 8]
            ext[f, x, 8:16, 0:128] = beside_y[f, 8 * x : 8 * x + 8]
            ext[f, x, 0:8, 128:256] = unpacked(beside_z[f], x)
            ext[f, x, 8:16, 128:256] = unpacked(corner[f], x)
    block = Block(arrays, None)
    block.faces_x(range(3, 10))
    block.faces(range(3, 11))
    block.weights(range(4, 10))
    block.relax(range(4, 10), block.ext, block.once)
    block.relax(range(5, 9), block.once, block.twice)
    block.coarse_parts(range(5, 9), parts)
    block.coarse_sums(list(range(5, 9)), parts, sums)


def outer_kernel(from_one, from_other, *refs):
    arrays, inner_sums = refs[:11], refs[11]
    smoothed_hbm, coarse = refs[12:14]
    outer = refs[14:25]
    parts, sums, smoothed, sem = refs[25:]
    ext = outer[0]
    gx, gy = lax.axis_index("gx"), lax.axis_index("gy")
    sub = iota((8, 128), 0)
    zero = jnp.zeros((8, 128), F32)

    def receive(pairs):
        for source, side in pairs:
            at = 0
            for d in range(3):
                plane = 11 + d if side else 2 - d
                for f in ALL:
                    into = f ^ 2 if f < 4 else f
                    if f in FIELDS_X[d]:
                        ext[into, plane, 0:8, 0:128] = source[at : at + 8]
                        at += 8
                    else:
                        ext[into, plane, 0:8, 0:128] = zero
            for f in ALL:
                into = f ^ 2 if f < 4 else f
                rows = source[at : at + 8]
                across = source[at + 72 : at + 80]
                at += 8
                lateral = roll(across, -48 if side else 48, 1)
                for d in range(3):
                    plane = 11 + d if side else 2 - d
                    slot = d if side else 7 - d
                    ext[into, plane, 0:8, 128:256] = unpacked(across, slot)
                    if d == 0:
                        ext[into, plane, 8:16, 0:128] = jnp.where((sub < 2) | (sub > 5), rows, 0.0)
                    elif d == 1:
                        ext[into, plane, 8:16, 0:128] = jnp.where((sub < 1) | (sub > 6), roll(rows, -3, 0), 0.0)
                    else:
                        ext[into, plane, 8:16, 0:128] = zero
                    ext[into, plane, 8:16, 128:256] = unpacked(lateral, slot) if d < 2 else zero

    by_side("gx", from_one, from_other, receive)
    block = Block(arrays, outer)
    block.faces_x((0, 1, 2, 10, 11, 12))
    block.faces((1, 2, 11, 12))
    block.weights((1, 2, 3, 10, 11, 12))
    block.relax((1, 2, 3, 10, 11, 12), block.ext, block.once)
    block.relax((2, 3, 4, 9, 10, 11), block.once, block.twice)

    rx_own, rx_low, rx_high = gx % 3, (gx + 2) % 3, (gx + 1) % 3
    ry_own, ry_low, ry_high = gy % 3, (gy + 2) % 3, (gy + 1) % 3
    for x in range(8):
        ids = block.cells(LAYER, x + 3, 8)[:, 0:128]
        residue = ids - 3.0 * jnp.floor((ids + 0.5) * (1.0 / 3.0))
        rx_other, rx_none = (rx_low, rx_high) if x < 4 else (rx_high, rx_low)
        for ex, rx in ((0, rx_own), (1, rx_other)):
            own = read(block.twice, x + 3, 2 * ex, 8)[:, 0:128]
            other = read(block.twice, x + 3, 2 * ex + 1, 8)[:, 0:128]
            low = jnp.where(sub < 4, other, 0.0)
            high = other - low
            for rz in range(3):
                hit = jnp.abs(residue - rz) < 0.5
                smoothed[9 * rz + 3 * ry_own + rx, x] = jnp.where(hit, own, 0.0)
                smoothed[9 * rz + 3 * ry_low + rx, x] = jnp.where(hit, low, 0.0)
                smoothed[9 * rz + 3 * ry_high + rx, x] = jnp.where(hit, high, 0.0)
        for rz in range(3):
            for ry in range(3):
                smoothed[9 * rz + 3 * ry + rx_none, x] = zero
    copy = pltpu.make_async_copy(smoothed, smoothed_hbm, sem)
    copy.start()

    block.coarse_parts((2, 3, 4, 9, 10, 11), parts)
    block.coarse_sums([2, 3, 4, 9, 10, 11], parts, sums)
    spot = iota((16, 256), 1)
    place = (jnp.where(spot < 192, spot, spot - 256) + 256) // BLOCK - 32
    for oz in range(3):
        total = jnp.zeros((16, 16), F32)
        for lift in range(2):
            rows = []
            for oy in range(3):
                for ox in range(3):
                    ey = 0 if oy == 1 else 1
                    value = sums[oz, lift, ox, ey] + inner_sums[oz, lift, ox, ey]
                    if oy != 1:
                        value = value[0:4] if oy == 0 else value[4:8]
                    rows.append(jnp.sum(value, axis=0, keepdims=True))
            rows.append(jnp.zeros((7, 256), F32))
            chosen = (place + lift - (oz - 1) == iota((16, 256), 0)).astype(F32)
            total = total + lax.dot_general(
                chosen,
                jnp.concatenate(rows, axis=0),
                (((1,), (1,)), ((), ())),
                precision=lax.Precision.HIGHEST,
                preferred_element_type=F32,
            )
        coarse[:, 9 * oz : 9 * oz + 9] = total[:, 0:9] * (1.0 / (BLOCK * BLOCK))
    copy.wait()


VMEM = pl.BlockSpec(memory_space=pltpu.VMEM)
HBM = pl.BlockSpec(memory_space=pltpu.HBM)


def call(kernel, outs, *operands, in_specs=None, out_specs=None, scratch=(), vmem=48 * 1024 * 1024):
    return pl.pallas_call(
        kernel,
        out_shape=[jax.ShapeDtypeStruct(shape, F32) for shape in outs],
        in_specs=in_specs or [VMEM] * len(operands),
        out_specs=out_specs or [VMEM] * len(outs),
        scratch_shapes=scratch,
        compiler_params=pltpu.CompilerParams(vmem_limit_bytes=vmem),
    )(*operands)


def exchange(axis, to_one, to_other):
    count = lax.axis_size(axis)
    one = [(i, i ^ 1) for i in range(count)]
    other = [(i, ((i + 1) ^ 1) - 1) for i in range(1, count - 1)]
    from_other = lax.ppermute(to_other, axis, other)
    return lax.ppermute(to_one, axis, one), from_other


def per_device(basis, perm, storage, layer):
    block = (FIELDS, 64, 128)
    side = (FIELDS, 8, 128)
    core, edge = call(
        pack_kernel,
        (block, side),
        basis.reshape(27, 64, 128),
        perm.reshape(3, 64, 128),
        storage.reshape(64, 128),
        layer.reshape(64, 128),
        in_specs=[HBM] * 4,
        vmem=None,
        scratch=[pltpu.VMEM((27, 64, 128), F32), pltpu.VMEM((64, 128), jnp.int32), pltpu.SemaphoreType.DMA((4,))],
    )
    one, other = exchange("gz", edge, edge)
    rows = (ROWS_Y + 32, 128)
    beside_z, to_one, to_other = call(y_kernel, (side, rows, rows), core, one, other)
    one, other = exchange("gy", to_one, to_other)
    rows = (ROWS_X + 144, 128)
    beside_y, corner, to_one, to_other = call(x_kernel, (block, side, rows, rows), core, beside_z, one, other)
    one, other = exchange("gx", to_one, to_other)

    def arrays(planes):
        return [
            (FIELDS, planes(3), 16, 256),
            (planes(3), 16, 256),
            (planes(3), 16, 256),
            (planes(3), 16, 256),
            (planes(3), 16, 256),
            (planes(3), 16, 256),
            (planes(3), 16, 256),
            (planes(3), 16, 256),
            (planes(4), 16, 256),
            (4, planes(4), 16, 256),
            (4, planes(5), 16, 256),
        ]

    parts = pltpu.VMEM((3, 2, 14, 16, 256), F32)
    sums = (3, 2, 3, 2, 8, 256)
    inner = call(
        inner_kernel, arrays(lambda first: 14 - 2 * first) + [sums], core, beside_z, beside_y, corner, scratch=[parts]
    )
    smoothed, coarse = call(
        outer_kernel,
        ((27, 8, 8, 128), (16, 27)),
        one,
        other,
        *inner,
        out_specs=[HBM, VMEM],
        scratch=[pltpu.VMEM(shape, F32) for shape in arrays(lambda first: 14)]
        + [parts, pltpu.VMEM(sums, F32), pltpu.VMEM((27, 8, 8, 128), F32), pltpu.SemaphoreType.DMA],
    )
    return smoothed, coarse.T.reshape(27, 1, 1, 16)


def solution(mesh):
    return jax.shard_map(
        per_device,
        mesh=mesh,
        in_specs=(
            P(None, "gx", "gy", "gz"),
            P(None, "gx", "gy", "gz"),
            P("gx", "gy", "gz"),
            P("gx", "gy", "gz"),
        ),
        out_specs=(P(None, "gx", "gy", "gz"), P(None, "gx", "gy", "gz")),
        check_vma=False,
    )
```

```python
import jax
import jax.numpy as jnp
from jax import lax
from jax.experimental import pallas as pl
from jax.experimental.pallas import tpu as pltpu
from jax.sharding import PartitionSpec as P

BLOCK = 8
FIELDS = 9
PX, PY, PZ, STORAGE, LAYER = 4, 5, 6, 7, 8
ALL = tuple(range(FIELDS))
FIELDS_X = (ALL, ALL, (0, 1, 2, 3, PX, LAYER))
FIELDS_Y = (ALL, ALL, (0, 1, 2, 3, PY, LAYER))
ROWS_Y = 8 * sum(len(f) for f in FIELDS_Y)
ROWS_X = 8 * sum(len(f) for f in FIELDS_X)
F32 = jnp.float32


def iota(shape, dim):
    return lax.broadcasted_iota(jnp.int32, shape, dim)


def roll(value, shift, axis):
    return pltpu.roll(value, shift % value.shape[axis], axis)


def pack_kernel(basis_hbm, perm_hbm, storage_hbm, layer_hbm, core_hbm, edge_hbm, core, edge, basis, layer, sems):
    copies = [
        pltpu.make_async_copy(source, target, sems.at[i])
        for i, (source, target) in enumerate(
            (
                (basis_hbm, basis),
                (layer_hbm, layer),
                (perm_hbm, core.at[PX : PZ + 1]),
                (storage_hbm, core.at[STORAGE]),
            )
        )
    ]
    for copy in copies:
        copy.start()
    gx, gy = lax.axis_index("gx"), lax.axis_index("gy")
    nx, ny = lax.axis_size("gx"), lax.axis_size("gy")
    sub, lane = iota((8, 128), 0), iota((8, 128), 1)
    rx_own, rx_low, rx_high = gx % 3, (gx + 2) % 3, (gx + 1) % 3
    ry_own, ry_low, ry_high = gy % 3, (gy + 2) % 3, (gy + 1) % 3
    low_rows = sub < 4
    y_valid = jnp.where(low_rows, (gy > 0).astype(F32), (gy < ny - 1).astype(F32))
    for copy in copies:
        copy.wait()
    ids = layer[...].astype(F32)
    core[LAYER] = ids
    residue = ids - 3.0 * jnp.floor((ids + 0.5) * (1.0 / 3.0))

    for x in range(8):
        here = residue[8 * x : 8 * x + 8]
        is_zero, is_one = here < 0.5, here < 1.5

        def at(rx, ry):
            first, second, third = (basis[9 * rz + 3 * ry + rx, 8 * x : 8 * x + 8] for rz in range(3))
            return jnp.where(is_zero, first, jnp.where(is_one, second, third))

        rx_other = rx_low if x < 4 else rx_high
        x_valid = ((gx > 0) if x < 4 else (gx < nx - 1)).astype(F32)
        for ex, rx in enumerate((rx_own, rx_other)):
            own = at(rx, ry_own)
            other = jnp.where(low_rows, at(rx, ry_low), at(rx, ry_high)) * y_valid
            if ex:
                own, other = own * x_valid, other * x_valid
            core[2 * ex, 8 * x : 8 * x + 8] = own
            core[2 * ex + 1, 8 * x : 8 * x + 8] = other
    keep = [pltpu.make_async_copy(core, core_hbm, sems.at[4]), pltpu.make_async_copy(edge, edge_hbm, sems.at[5])]
    keep[0].start()
    for f in ALL:
        packed = jnp.zeros((8, 128), F32)
        for x in range(8):
            value = core[f, 8 * x : 8 * x + 8]
            value = jnp.where(lane < 4, value, roll(value, 16, 1))
            packed = jnp.where(lane // 16 == x, roll(value, 16 * x, 1), packed)
        edge[f] = packed
    keep[1].start()
    for copy in keep:
        copy.wait()


def load_kernel(core_hbm, core):
    core[...] = core_hbm[...]


def by_side(axis, one, other, body):
    even = lax.axis_index(axis) % 2 == 0
    pl.when(even)(lambda: body(((one, 1), (other, 0))))
    pl.when(jnp.logical_not(even))(lambda: body(((one, 0), (other, 1))))


def y_kernel(core, from_one, from_other, beside_z, to_one, to_other):
    lane = iota((8, 128), 1)
    high = (lane % 16 < 4).astype(jnp.int32)
    odd = lax.axis_index("gz") % 2
    for f in ALL:
        beside_z[f] = jnp.where(high != odd, from_one[f], from_other[f])

    def send(pairs):
        for out, side in pairs:
            at = 0
            for d, fields in enumerate(FIELDS_Y):
                y = 7 - d if side else d
                for f in fields:
                    out[at : at + 8] = core[f, pl.ds(y, 8, stride=8), :]
                    at += 8
            for d in range(3):
                y = 7 - d if side else d
                for f in ALL:
                    out[at : at + 1] = beside_z[f, y : y + 1]
                    at += 1

    by_side("gy", to_one, to_other, send)


def x_kernel(core, beside_z, from_one, from_other, beside_y, corner, to_one, to_other):
    sub, lane = iota((8, 128), 0), iota((8, 128), 1)
    beside_y[...] = jnp.zeros(beside_y.shape, F32)
    corner[...] = jnp.zeros(corner.shape, F32)

    def receive(pairs):
        for source, side in pairs:
            at = 0
            for d, fields in enumerate(FIELDS_Y):
                row = d if side else 7 - d
                for f in fields:
                    into = f ^ 1 if f < 4 else f
                    beside_y[into, pl.ds(row, 8, stride=8), :] = source[at : at + 8]
                    at += 8
            for d in range(3):
                row = d if side else 7 - d
                for f in ALL:
                    into = f ^ 1 if f < 4 else f
                    corner[into, row : row + 1] = source[at : at + 1]
                    at += 1

    by_side("gy", from_one, from_other, receive)

    def send(pairs):
        for out, side in pairs:
            at = 0
            for d, fields in enumerate(FIELDS_X):
                x = 7 - d if side else d
                for f in fields:
                    out[at : at + 8] = core[f, 8 * x : 8 * x + 8]
                    at += 8
            first, second = (7, 6) if side else (0, 1)
            for f in ALL:
                out[at : at + 8] = jnp.where(
                    (sub == 2) | (sub == 3),
                    roll(beside_y[f, 8 * second : 8 * second + 8], 3, 0),
                    beside_y[f, 8 * first : 8 * first + 8],
                )
                at += 8
            for f in ALL:
                out[at : at + 8] = jnp.where(
                    (lane >= 48) & (lane < 80), roll(corner[f], -48 if side else 48, 1), beside_z[f]
                )
                at += 8

    by_side("gx", to_one, to_other, send)


def harmonic(first, second):
    total = first + second
    return 2.0 * first * second / jnp.where(total > 0.0, total, 1.0)


def unpacked(value, slot):
    lane = iota((8, 128), 1)
    value = roll(value, -16 * slot, 1)
    return jnp.where(lane < 3, value, jnp.where(lane >= 117, roll(value, 112, 1), 0.0))


class Planes:
    def __init__(self, inner, outer, first):
        self.inner, self.outer, self.first, self.last = inner, outer, first, 13 - first

    def at(self, p, shift=0):
        if self.first <= p <= self.last - shift:
            return self.inner, p - self.first
        return self.outer, p


def read(planes, p, f=None, tall=16, shift=0):
    ref, p = planes.at(p, shift)
    return ref[p, 0:tall] if f is None else ref[f, p, 0:tall]


def write(planes, value, p, f=None, shift=0):
    ref, p = planes.at(p, shift)
    rows = value.shape[0]
    if f is None:
        ref[p, 0:rows] = value
    else:
        ref[f, p, 0:rows] = value


class Block:
    def __init__(self, inner, outer):
        names = ("ext", "face_x", "near_x", "face_y", "face_z", "near_y", "near_z", "rest", "weight", "once", "twice")
        first = (3, 3, 3, 3, 3, 3, 3, 3, 4, 4, 5)
        for i, name in enumerate(names):
            setattr(self, name, Planes(inner[i], outer[i] if outer else None, first[i]))
        self.row, self.column = iota((16, 256), 0), iota((16, 256), 1)

    def cells(self, f, p, tall=16):
        return read(self.ext, p, f, tall)

    def side_x(self, planes, p, tall=16):
        return read(planes, p, None, tall, 1)

    def faces_x(self, planes):
        for p in planes:
            face = harmonic(self.cells(PX, p), self.cells(PX, p + 1))
            write(self.face_x, face, p, None, 1)
            write(self.near_x, jnp.where(self.cells(LAYER, p) == self.cells(LAYER, p + 1), face, 0.0), p, None, 1)

    def faces(self, planes):
        for p in planes:
            ids = self.cells(LAYER, p)
            total = self.cells(STORAGE, p)
            for f, axis, face_at, near_at in ((PY, 0, self.face_y, self.near_y), (PZ, 1, self.face_z, self.near_z)):
                across = self.cells(f, p)
                face = harmonic(across, roll(across, -1, axis))
                write(face_at, face, p)
                write(near_at, jnp.where(ids == roll(ids, -1, axis), face, 0.0), p)
                total = total + (face + roll(face, 1, axis))
            write(self.rest, total, p)

    def diagonal(self, p):
        return read(self.rest, p) + (self.side_x(self.face_x, p - 1) + self.side_x(self.face_x, p))

    def weights(self, planes):
        for p in planes:
            total = self.diagonal(p)
            write(self.weight, (2.0 / 3.0) / jnp.where(total > 0.0, total, 1.0), p)

    def height(self, p, source):
        return 8 if p in ((1, 12) if source is self.ext else (2, 11)) else 16

    def beside(self, p, source, low=True, high=True):
        tall = self.height(p, source)
        near_y, near_z = read(self.near_y, p), read(self.near_z, p, None, tall)
        near_y_other = jnp.where(self.row == 3, 0.0, near_y)
        totals = []
        for f in range(4):
            whole = read(source, p, f)
            own = whole[0:tall]
            side = near_y_other if f & 1 else near_y
            total = side[0:tall] * roll(whole, -1, 0)[0:tall] + roll(side * whole, 1, 0)[0:tall]
            totals.append(total + (near_z * roll(own, -1, 1) + roll(near_z * own, 1, 1)))
        return self.beside_x(p, source, totals, low, high)

    def beside_x(self, p, source, totals, low=False, high=False):
        tall = self.height(p, source)
        totals = list(totals)
        if low:
            face = self.side_x(self.near_x, p - 1, tall)
            for f in range(2 if p == 7 else 4):
                totals[f] = totals[f] + face * read(source, p - 1, f, tall)
        if high:
            face = self.side_x(self.near_x, p, tall)
            for f in range(2 if p == 6 else 4):
                totals[f] = totals[f] + face * read(source, p + 1, f, tall)
        return totals

    def relax(self, p, source, target, totals):
        gx, gy = lax.axis_index("gx"), lax.axis_index("gy")
        nx, ny = lax.axis_size("gx"), lax.axis_size("gy")
        tall = self.height(p, source)
        row = self.row[0:tall]
        y_valid = jnp.where((row < 4) | (row >= 12), (gy > 0).astype(F32), (gy < ny - 1).astype(F32))
        x_valid = ((gx > 0) if p < 7 else (gx < nx - 1)).astype(F32)
        scale = read(self.weight, p, None, tall)
        scale_other = scale * y_valid
        updated = []
        for f in range(4):
            factor = scale_other if f & 1 else scale
            if f & 2:
                factor = factor * x_valid
            updated.append(read(source, p, f, tall) * (1.0 / 3.0) + factor * totals[f])
        total = (updated[0] + updated[1]) + (updated[2] + updated[3])
        inverse = 1.0 / jnp.where(total > 0.0, total, 1.0)
        for f in range(4):
            write(target, updated[f] * inverse, p, f)

    def sweep(self, planes, source, target):
        for p in planes:
            self.relax(p, source, target, self.beside(p, source))

    def coarse_parts(self, planes, parts):
        row = self.row
        octet = self.octets()
        in_block = row < 8
        for p in planes:
            inside = 3 <= p <= 10
            tall = 16 if inside else 8
            ids = self.cells(LAYER, p, tall)
            lifted = ids > octet[0:tall]
            keep = in_block[0:tall]
            given = []
            if p >= 4:
                given.append((self.side_x(self.face_x, p - 1, tall), self.cells(LAYER, p - 1, tall), keep))
            if p <= 9:
                given.append((self.side_x(self.face_x, p, tall), self.cells(LAYER, p + 1, tall), keep))
            total = [jnp.zeros((tall, 256), F32) for _ in range(3)]
            if inside:
                face = read(self.face_y, p)
                given.append((face, roll(ids, -1, 0), (row < 7) | (row == 15)))
                given.append((roll(face, 1, 0), roll(ids, 1, 0), (row > 0) & (row < 9)))
                face = read(self.face_z, p)
                given.append((face, roll(ids, -1, 1), keep))
                given.append((roll(face, 1, 1), roll(ids, 1, 1), keep))
                own = read(self.rest, p)
                if p >= 4:
                    own = own + self.side_x(self.face_x, p - 1)
                if p <= 9:
                    own = own + self.side_x(self.face_x, p)
                total[1] = jnp.where(keep, own, 0.0)
            for face, beside, kept in given:
                face = jnp.where(kept, face, 0.0)
                step = beside - ids
                total[0] = total[0] - jnp.where(step == 1.0, face, 0.0)
                total[1] = total[1] - jnp.where(step == 0.0, face, 0.0)
                total[2] = total[2] - jnp.where(step == -1.0, face, 0.0)
            for oz in range(3):
                upper = jnp.where(lifted, total[oz], 0.0)
                ref, at = parts.at(p)
                ref[oz, 0, at, 0:tall] = total[oz] - upper
                ref[oz, 1, at, 0:tall] = upper

    def coarse_outer_faces(self, parts, outer_parts):
        row, octet = self.row, self.octets()
        for p, face in ((3, 2), (10, 10)):
            face = jnp.where(row < 8, self.side_x(self.face_x, face), 0.0)
            upper = jnp.where(self.cells(LAYER, p) > octet, face, 0.0)
            ref, at = parts.at(p)
            outer_parts[1, 0, p] = ref[1, 0, at] + (face - upper)
            outer_parts[1, 1, p] = ref[1, 1, at] + upper

    def octets(self):
        octet = (jnp.where(self.column < 192, self.column, self.column - 256) + 256) // BLOCK - 32
        return (octet + lax.axis_index("gz") * (128 // BLOCK)).astype(F32)

    def coarse_sums(self, planes, parts, sums, changed=None):
        for oz in range(3):
            for lift in range(2):
                for f in range(4):
                    groups = (planes,) if f < 2 else ([p for p in planes if p < 7], [p for p in planes if p >= 7])
                    for i, group in enumerate(groups):
                        top = bottom = None
                        for p in group:
                            part, spot = parts.at(p)
                            if changed is not None and oz == 1 and p in (3, 10):
                                part, spot = changed, p
                            value = part[oz, lift, spot, 0:8] * read(self.twice, p, f, 8)
                            top = value if top is None else top + value
                            if 3 <= p <= 10:
                                ref, at = self.twice.at(p)
                                value = part[oz, lift, spot, 8:16] * ref[f, at, 8:16]
                                bottom = value if bottom is None else bottom + value
                        ox = 1 if f < 2 else 2 * i
                        sums[oz, lift, ox, f & 1] = top + (roll(bottom, 4, 0) if f & 1 else bottom)


def store_slots(block, planes, smoothed):
    gx, gy = lax.axis_index("gx"), lax.axis_index("gy")
    rx_own, rx_low, rx_high = gx % 3, (gx + 2) % 3, (gx + 1) % 3
    ry_own, ry_low, ry_high = gy % 3, (gy + 2) % 3, (gy + 1) % 3
    sub = iota((8, 128), 0)
    zero = jnp.zeros((8, 128), F32)
    for i, x in enumerate(planes):
        ids = block.cells(LAYER, x + 3, 8)[:, 0:128]
        residue = ids - 3.0 * jnp.floor((ids + 0.5) * (1.0 / 3.0))
        rx_other, rx_none = (rx_low, rx_high) if x < 4 else (rx_high, rx_low)
        for ex, rx in ((0, rx_own), (1, rx_other)):
            own = read(block.twice, x + 3, 2 * ex, 8)[:, 0:128]
            other = read(block.twice, x + 3, 2 * ex + 1, 8)[:, 0:128]
            low = jnp.where(sub < 4, other, 0.0)
            high = other - low
            for rz in range(3):
                hit = jnp.abs(residue - rz) < 0.5
                smoothed[9 * rz + 3 * ry_own + rx, i] = jnp.where(hit, own, 0.0)
                smoothed[9 * rz + 3 * ry_low + rx, i] = jnp.where(hit, low, 0.0)
                smoothed[9 * rz + 3 * ry_high + rx, i] = jnp.where(hit, high, 0.0)
        for rz in range(3):
            for ry in range(3):
                smoothed[9 * rz + 3 * ry + rx_none, i] = zero


def inner_kernel(core, beside_z, beside_y, corner, *refs):
    arrays, (sums, parts_ref, held_once, held_twice, smoothed_hbm) = refs[:11], refs[11:16]
    smoothed, sem = refs[16:]
    ext = arrays[0]
    for f in ALL:
        for x in range(8):
            ext[f, x, 0:8, 0:128] = core[f, 8 * x : 8 * x + 8]
            ext[f, x, 8:16, 0:128] = beside_y[f, 8 * x : 8 * x + 8]
            ext[f, x, 0:8, 128:256] = unpacked(beside_z[f], x)
            ext[f, x, 8:16, 128:256] = unpacked(corner[f], x)
    block = Block(arrays, None)
    parts = Planes(parts_ref, None, 3)
    block.faces_x(range(3, 10))
    block.faces(range(3, 11))
    block.weights(range(4, 10))
    block.sweep(range(4, 10), block.ext, block.once)
    block.sweep(range(5, 9), block.once, block.twice)
    store_slots(block, (2, 3, 4, 5), smoothed)
    copy = pltpu.make_async_copy(smoothed, smoothed_hbm.at[:, 2:6], sem)
    copy.start()
    for held, source, first, last in ((held_once, block.ext, 3, 10), (held_twice, block.once, 4, 9)):
        for i, p in enumerate((first, last)):
            for f, total in enumerate(block.beside(p, source, low=i == 1, high=i == 0)):
                held[f, i] = total
    block.coarse_parts(range(3, 11), parts)
    block.coarse_sums(list(range(5, 9)), parts, sums)
    copy.wait()


def outer_kernel(from_one, from_other, *refs):
    arrays, (inner_sums, inner_parts, held_once, held_twice, _) = refs[:11], refs[11:16]
    smoothed_hbm, coarse = refs[16:18]
    outer = refs[18:29]
    outer_parts, sums, smoothed, sem = refs[29:]
    ext = outer[0]
    sub = iota((8, 128), 0)
    zero = jnp.zeros((8, 128), F32)

    def receive(pairs):
        for source, side in pairs:
            at = 0
            for d in range(3):
                plane = 11 + d if side else 2 - d
                for f in ALL:
                    into = f ^ 2 if f < 4 else f
                    if f in FIELDS_X[d]:
                        ext[into, plane, 0:8, 0:128] = source[at : at + 8]
                        at += 8
                    else:
                        ext[into, plane, 0:8, 0:128] = zero
            for f in ALL:
                into = f ^ 2 if f < 4 else f
                rows = source[at : at + 8]
                across = source[at + 72 : at + 80]
                at += 8
                lateral = roll(across, -48 if side else 48, 1)
                for d in range(3):
                    plane = 11 + d if side else 2 - d
                    slot = d if side else 7 - d
                    ext[into, plane, 0:8, 128:256] = unpacked(across, slot)
                    if d == 0:
                        ext[into, plane, 8:16, 0:128] = jnp.where((sub < 2) | (sub > 5), rows, 0.0)
                    elif d == 1:
                        ext[into, plane, 8:16, 0:128] = jnp.where((sub < 1) | (sub > 6), roll(rows, -3, 0), 0.0)
                    else:
                        ext[into, plane, 8:16, 0:128] = zero
                    ext[into, plane, 8:16, 128:256] = unpacked(lateral, slot) if d < 2 else zero

    by_side("gx", from_one, from_other, receive)
    block = Block(arrays, outer)
    block.faces_x((0, 1, 2, 10, 11, 12))
    block.faces((1, 2, 11, 12))
    block.weights((1, 2, 3, 10, 11, 12))
    steps = (
        (held_once, block.ext, block.once, (1, 2, 11, 12), (3, 10)),
        (held_twice, block.once, block.twice, (2, 3, 10, 11), (4, 9)),
    )
    for held, source, target, whole, begun in steps:
        block.sweep(whole, source, target)
        for i, p in enumerate(begun):
            totals = block.beside_x(p, source, [held[f, i] for f in range(4)], low=i == 0, high=i == 1)
            block.relax(p, source, target, totals)
    store_slots(block, (0, 1, 6, 7), smoothed)
    copies = [
        pltpu.make_async_copy(smoothed.at[:, 0:2], smoothed_hbm.at[:, 0:2], sem.at[0]),
        pltpu.make_async_copy(smoothed.at[:, 2:4], smoothed_hbm.at[:, 6:8], sem.at[1]),
    ]
    for copy in copies:
        copy.start()

    parts = Planes(inner_parts, outer_parts, 3)
    block.coarse_parts((2, 11), parts)
    block.coarse_outer_faces(parts, outer_parts)
    block.coarse_sums([2, 3, 4, 9, 10, 11], parts, sums, outer_parts)
    spot = iota((16, 256), 1)
    place = (jnp.where(spot < 192, spot, spot - 256) + 256) // BLOCK - 32
    for oz in range(3):
        total = jnp.zeros((16, 16), F32)
        for lift in range(2):
            rows = []
            for oy in range(3):
                for ox in range(3):
                    ey = 0 if oy == 1 else 1
                    value = sums[oz, lift, ox, ey] + inner_sums[oz, lift, ox, ey]
                    if oy != 1:
                        value = value[0:4] if oy == 0 else value[4:8]
                    rows.append(jnp.sum(value, axis=0, keepdims=True))
            rows.append(jnp.zeros((7, 256), F32))
            chosen = (place + lift - (oz - 1) == iota((16, 256), 0)).astype(F32)
            total = total + lax.dot_general(
                chosen,
                jnp.concatenate(rows, axis=0),
                (((1,), (1,)), ((), ())),
                precision=lax.Precision.HIGHEST,
                preferred_element_type=F32,
            )
        coarse[:, 9 * oz : 9 * oz + 9] = total[:, 0:9] * (1.0 / (BLOCK * BLOCK))
    for copy in copies:
        copy.wait()


VMEM = pl.BlockSpec(memory_space=pltpu.VMEM)
HBM = pl.BlockSpec(memory_space=pltpu.HBM)


def call(kernel, outs, *operands, in_specs=None, out_specs=None, scratch=(), aliases=None, vmem=48 * 1024 * 1024):
    return pl.pallas_call(
        kernel,
        out_shape=[jax.ShapeDtypeStruct(shape, F32) for shape in outs],
        in_specs=in_specs or [VMEM] * len(operands),
        out_specs=out_specs or [VMEM] * len(outs),
        scratch_shapes=scratch,
        input_output_aliases=aliases or {},
        compiler_params=pltpu.CompilerParams(vmem_limit_bytes=vmem),
    )(*operands)


def exchange(axis, to_one, to_other):
    count = lax.axis_size(axis)
    one = [(i, i ^ 1) for i in range(count)]
    other = [(i, ((i + 1) ^ 1) - 1) for i in range(1, count - 1)]
    from_other = lax.ppermute(to_other, axis, other)
    return lax.ppermute(to_one, axis, one), from_other


def per_device(basis, perm, storage, layer):
    block = (FIELDS, 64, 128)
    side = (FIELDS, 8, 128)
    core, edge = call(
        pack_kernel,
        (block, side),
        basis.reshape(27, 64, 128),
        perm.reshape(3, 64, 128),
        storage.reshape(64, 128),
        layer.reshape(64, 128),
        in_specs=[HBM] * 4,
        out_specs=[HBM, HBM],
        vmem=None,
        scratch=[
            pltpu.VMEM(block, F32),
            pltpu.VMEM(side, F32),
            pltpu.VMEM((27, 64, 128), F32),
            pltpu.VMEM((64, 128), jnp.int32),
            pltpu.SemaphoreType.DMA((6,)),
        ],
    )
    one, other = exchange("gz", edge, edge)
    (core,) = call(load_kernel, (block,), core)
    rows = (ROWS_Y + 32, 128)
    beside_z, to_one, to_other = call(y_kernel, (side, rows, rows), core, one, other)
    one, other = exchange("gy", to_one, to_other)
    rows = (ROWS_X + 144, 128)
    beside_y, corner, to_one, to_other = call(x_kernel, (block, side, rows, rows), core, beside_z, one, other)
    one, other = exchange("gx", to_one, to_other)

    def arrays(planes):
        return [
            (FIELDS, planes(3), 16, 256),
            (planes(3), 16, 256),
            (planes(3), 16, 256),
            (planes(3), 16, 256),
            (planes(3), 16, 256),
            (planes(3), 16, 256),
            (planes(3), 16, 256),
            (planes(3), 16, 256),
            (planes(4), 16, 256),
            (4, planes(4), 16, 256),
            (4, planes(5), 16, 256),
        ]

    sums = (3, 2, 3, 2, 8, 256)
    whole = (27, 8, 8, 128)
    half = pltpu.VMEM((27, 4, 8, 128), F32)
    held = (4, 2, 16, 256)
    outs = arrays(lambda first: 14 - 2 * first) + [sums, (3, 2, 8, 16, 256), held, held, whole]
    inner = call(
        inner_kernel,
        outs,
        core,
        beside_z,
        beside_y,
        corner,
        out_specs=[VMEM] * 15 + [HBM],
        scratch=[half, pltpu.SemaphoreType.DMA],
    )
    smoothed, coarse = call(
        outer_kernel,
        (whole, (16, 27)),
        one,
        other,
        *inner,
        in_specs=[VMEM] * 17 + [HBM],
        out_specs=[HBM, VMEM],
        scratch=[pltpu.VMEM(shape, F32) for shape in arrays(lambda first: 14)]
        + [pltpu.VMEM((3, 2, 14, 16, 256), F32), pltpu.VMEM(sums, F32), half, pltpu.SemaphoreType.DMA((2,))],
        aliases={17: 0},
    )
    return smoothed, coarse.T.reshape(27, 1, 1, 16)


def solution(mesh):
    return jax.shard_map(
        per_device,
        mesh=mesh,
        in_specs=(
            P(None, "gx", "gy", "gz"),
            P(None, "gx", "gy", "gz"),
            P("gx", "gy", "gz"),
            P("gx", "gy", "gz"),
        ),
        out_specs=(P(None, "gx", "gy", "gz"), P(None, "gx", "gy", "gz")),
        check_vma=False,
    )
```

```python
import jax
import jax.numpy as jnp
from jax import lax
from jax.experimental import pallas as pl
from jax.experimental.pallas import tpu as pltpu
from jax.sharding import PartitionSpec as P

BLOCK = 8
FIELDS = 9
PX, PY, PZ, STORAGE, LAYER = 4, 5, 6, 7, 8
ALL = tuple(range(FIELDS))
FIELDS_X = (ALL, ALL, (0, 1, 2, 3, PX, LAYER))
FIELDS_Y = (ALL, ALL, (0, 1, 2, 3, PY, LAYER))
ROWS_Y = 8 * sum(len(f) for f in FIELDS_Y)
ROWS_X = 8 * sum(len(f) for f in FIELDS_X)
FIELDS_XY = (0, 1, 2, 3, PX, PY, LAYER)
ROWS_XY = (
    [(0, row, f) for row in (7, 0) for f in ALL]
    + [(0, row, f) for row in (6, 1) for f in FIELDS_XY]
    + [(1, row, f) for row in (7, 0) for f in FIELDS_XY]
)
F32 = jnp.float32


def iota(shape, dim):
    return lax.broadcasted_iota(jnp.int32, shape, dim)


def roll(value, shift, axis):
    return pltpu.roll(value, shift % value.shape[axis], axis)


def pack_kernel(basis_hbm, perm_hbm, storage_hbm, layer_hbm, core_hbm, edge_hbm, core, edge, basis, layer, sems):
    rest = [
        pltpu.make_async_copy(layer_hbm, layer, sems.at[0]),
        pltpu.make_async_copy(perm_hbm, core.at[PX : PZ + 1], sems.at[1]),
        pltpu.make_async_copy(storage_hbm, core.at[STORAGE], sems.at[2]),
    ]
    arriving = pltpu.make_async_copy(basis_hbm, basis, sems.at[3])
    for copy in rest + [arriving]:
        copy.start()
    gx, gy = lax.axis_index("gx"), lax.axis_index("gy")
    nx, ny = lax.axis_size("gx"), lax.axis_size("gy")
    sub, lane = iota((8, 128), 0), iota((8, 128), 1)
    rx_own, rx_low, rx_high = gx % 3, (gx + 2) % 3, (gx + 1) % 3
    ry_own, ry_low, ry_high = gy % 3, (gy + 2) % 3, (gy + 1) % 3
    low_rows = sub < 4
    y_valid = jnp.where(low_rows, (gy > 0).astype(F32), (gy < ny - 1).astype(F32))

    def moved(value, x):
        return roll(jnp.where(lane < 4, value, roll(value, 16, 1)), 16 * x, 1)

    for copy in rest:
        copy.wait()
    ids = layer[...].astype(F32)
    core[LAYER] = ids
    kept = [pltpu.make_async_copy(core.at[4:9], core_hbm.at[4:9], sems.at[4])]
    kept[0].start()
    residue = ids - 3.0 * jnp.floor((ids + 0.5) * (1.0 / 3.0))
    strip = lane // 16
    for f in range(4, FIELDS):
        packed = jnp.zeros((8, 128), F32)
        for x in range(8):
            packed = jnp.where(strip == x, moved(core[f, 8 * x : 8 * x + 8], x), packed)
        edge[f] = packed

    packed = [jnp.zeros((8, 128), F32) for _ in range(4)]
    arriving.wait()
    for x in range(8):
        here = residue[8 * x : 8 * x + 8]
        is_zero, is_one = here < 0.5, here < 1.5

        def at(rx, ry):
            first, second, third = (basis[9 * rz + 3 * ry + rx, 8 * x : 8 * x + 8] for rz in range(3))
            return jnp.where(is_zero, first, jnp.where(is_one, second, third))

        rx_other = rx_low if x < 4 else rx_high
        x_valid = ((gx > 0) if x < 4 else (gx < nx - 1)).astype(F32)
        for ex, rx in enumerate((rx_own, rx_other)):
            own = at(rx, ry_own)
            other = jnp.where(low_rows, at(rx, ry_low), at(rx, ry_high)) * y_valid
            if ex:
                own, other = own * x_valid, other * x_valid
            for f, value in ((2 * ex, own), (2 * ex + 1, other)):
                core[f, 8 * x : 8 * x + 8] = value
                packed[f] = jnp.where(strip == x, moved(value, x), packed[f])
    for f in range(4):
        edge[f] = packed[f]
    kept.append(pltpu.make_async_copy(edge, edge_hbm, sems.at[5]))
    kept.append(pltpu.make_async_copy(core.at[0:4], core_hbm.at[0:4], sems.at[6]))
    kept[1].start()
    kept[2].start()
    for copy in kept:
        copy.wait()


def load_kernel(core_hbm, core):
    core[...] = core_hbm[...]


def by_side(axis, one, other, body):
    even = lax.axis_index(axis) % 2 == 0
    pl.when(even)(lambda: body(((one, 0), (other, 1))))
    pl.when(jnp.logical_not(even))(lambda: body(((one, 1), (other, 0))))


def y_kernel(core, from_one, from_other, beside_z, to_one, to_other):
    lane = iota((8, 128), 1)
    high = (lane % 16 < 4).astype(jnp.int32)
    odd = lax.axis_index("gz") % 2
    for f in ALL:
        beside_z[f] = jnp.where(high != odd, from_one[f], from_other[f])

    def send(pairs):
        for out, side in pairs:
            at = 0
            for d, fields in enumerate(FIELDS_Y):
                y = 7 - d if side else d
                for f in fields:
                    out[at : at + 8] = core[f, pl.ds(y, 8, stride=8), :]
                    at += 8
            for d, fields in enumerate(FIELDS_Y):
                y = 7 - d if side else d
                for f in fields:
                    out[at : at + 1] = beside_z[f, y : y + 1]
                    at += 1

    by_side("gy", to_one, to_other, send)


def x_kernel(core, beside_z, from_one, from_other, beside_y, corner, to_one, to_other):
    lane = iota((8, 128), 1)
    zero = jnp.zeros((8, 128), F32)
    beside_y[...] = jnp.zeros(beside_y.shape, F32)
    corner[...] = jnp.zeros(corner.shape, F32)

    def receive(pairs):
        for source, side in pairs:
            at = 0
            for d, fields in enumerate(FIELDS_Y):
                row = d if side else 7 - d
                for f in fields:
                    into = f ^ 1 if f < 4 else f
                    beside_y[into, pl.ds(row, 8, stride=8), :] = source[at : at + 8]
                    at += 8
            for d, fields in enumerate(FIELDS_Y):
                row = d if side else 7 - d
                for f in fields:
                    into = f ^ 1 if f < 4 else f
                    corner[into, row : row + 1] = source[at : at + 1]
                    at += 1

    by_side("gy", from_one, from_other, receive)

    def send(pairs):
        for out, side in pairs:
            at = 0
            for d, fields in enumerate(FIELDS_X):
                x = 7 - d if side else d
                for f in fields:
                    out[at : at + 8] = core[f, 8 * x : 8 * x + 8]
                    at += 8
            for d, row, f in ROWS_XY:
                from_row = 8 * (7 - d if side else d) + row
                out[at : at + 1] = beside_y[f, from_row : from_row + 1]
                at += 1
            out[at : at + 2] = jnp.zeros((2, 128), F32)
            at += 2
            strips = []
            for f in ALL:
                value = jnp.where((lane >= 48) & (lane < 80), roll(corner[f], -48 if side else 48, 1), beside_z[f])
                strips.append(roll(value, 80 * f - 48 * side, 1))
            for v in range(6):
                value = zero
                for f in ALL:
                    start, stop = max(5 * f, 8 * v), min(5 * f + 5, 8 * v + 8)
                    if start < stop:
                        inside = (lane >= 16 * (start - 8 * v)) & (lane < 16 * (stop - 8 * v))
                        value = jnp.where(inside, strips[f], value)
                out[at : at + 8] = value
                at += 8

    by_side("gx", to_one, to_other, send)


def harmonic(first, second):
    total = first + second
    return 2.0 * first * second / jnp.where(total > 0.0, total, 1.0)


def unpacked(value, slot):
    lane = iota((8, 128), 1)
    value = roll(value, -16 * slot, 1)
    return jnp.where(lane < 3, value, jnp.where(lane >= 117, roll(value, 112, 1), 0.0))


class Planes:
    def __init__(self, inner, outer, first):
        self.inner, self.outer, self.first, self.last = inner, outer, first, 13 - first

    def at(self, p, shift=0):
        if self.first <= p <= self.last - shift:
            return self.inner, p - self.first
        return self.outer, p


def read(planes, p, f=None, tall=16, shift=0):
    ref, p = planes.at(p, shift)
    return ref[p, 0:tall] if f is None else ref[f, p, 0:tall]


def write(planes, value, p, f=None, shift=0):
    ref, p = planes.at(p, shift)
    rows = value.shape[0]
    if f is None:
        ref[p, 0:rows] = value
    else:
        ref[f, p, 0:rows] = value


class Block:
    def __init__(self, inner, outer):
        names = ("ext", "face_x", "near_x", "face_y", "face_z", "near_y", "near_z", "rest", "weight", "once", "twice")
        first = (3, 3, 3, 3, 3, 3, 3, 3, 4, 4, 5)
        for i, name in enumerate(names):
            setattr(self, name, Planes(inner[i], outer[i] if outer else None, first[i]))
        self.row, self.column = iota((16, 256), 0), iota((16, 256), 1)

    def cells(self, f, p, tall=16):
        return read(self.ext, p, f, tall)

    def side_x(self, planes, p, tall=16):
        return read(planes, p, None, tall, 1)

    def faces_x(self, planes):
        for p in planes:
            face = harmonic(self.cells(PX, p), self.cells(PX, p + 1))
            write(self.face_x, face, p, None, 1)
            write(self.near_x, jnp.where(self.cells(LAYER, p) == self.cells(LAYER, p + 1), face, 0.0), p, None, 1)

    def faces(self, planes):
        for p in planes:
            ids = self.cells(LAYER, p)
            total = self.cells(STORAGE, p)
            for f, axis, face_at, near_at in ((PY, 0, self.face_y, self.near_y), (PZ, 1, self.face_z, self.near_z)):
                across = self.cells(f, p)
                face = harmonic(across, roll(across, -1, axis))
                write(face_at, face, p)
                write(near_at, jnp.where(ids == roll(ids, -1, axis), face, 0.0), p)
                total = total + (face + roll(face, 1, axis))
            write(self.rest, total, p)

    def diagonal(self, p):
        return read(self.rest, p) + (self.side_x(self.face_x, p - 1) + self.side_x(self.face_x, p))

    def weights(self, planes):
        for p in planes:
            total = self.diagonal(p)
            write(self.weight, (2.0 / 3.0) / jnp.where(total > 0.0, total, 1.0), p)

    def height(self, p, source):
        return 8 if p in ((1, 12) if source is self.ext else (2, 11)) else 16

    def beside(self, p, source, low=True, high=True):
        tall = self.height(p, source)
        near_y, near_z = read(self.near_y, p), read(self.near_z, p, None, tall)
        near_y_other = jnp.where(self.row == 3, 0.0, near_y)
        totals = []
        for f in range(4):
            whole = read(source, p, f)
            own = whole[0:tall]
            side = near_y_other if f & 1 else near_y
            total = side[0:tall] * roll(whole, -1, 0)[0:tall] + roll(side * whole, 1, 0)[0:tall]
            totals.append(total + (near_z * roll(own, -1, 1) + roll(near_z * own, 1, 1)))
        return self.beside_x(p, source, totals, low, high)

    def beside_x(self, p, source, totals, low=False, high=False):
        tall = self.height(p, source)
        totals = list(totals)
        if low:
            face = self.side_x(self.near_x, p - 1, tall)
            for f in range(2 if p == 7 else 4):
                totals[f] = totals[f] + face * read(source, p - 1, f, tall)
        if high:
            face = self.side_x(self.near_x, p, tall)
            for f in range(2 if p == 6 else 4):
                totals[f] = totals[f] + face * read(source, p + 1, f, tall)
        return totals

    def relax(self, p, source, target, totals):
        gx, gy = lax.axis_index("gx"), lax.axis_index("gy")
        nx, ny = lax.axis_size("gx"), lax.axis_size("gy")
        tall = self.height(p, source)
        row = self.row[0:tall]
        y_valid = jnp.where((row < 4) | (row >= 12), (gy > 0).astype(F32), (gy < ny - 1).astype(F32))
        x_valid = ((gx > 0) if p < 7 else (gx < nx - 1)).astype(F32)
        scale = read(self.weight, p, None, tall)
        scale_other = scale * y_valid
        updated = []
        for f in range(4):
            factor = scale_other if f & 1 else scale
            if f & 2:
                factor = factor * x_valid
            updated.append(read(source, p, f, tall) * (1.0 / 3.0) + factor * totals[f])
        total = (updated[0] + updated[1]) + (updated[2] + updated[3])
        inverse = 1.0 / jnp.where(total > 0.0, total, 1.0)
        for f in range(4):
            write(target, updated[f] * inverse, p, f)

    def sweep(self, planes, source, target):
        for p in planes:
            self.relax(p, source, target, self.beside(p, source))

    def coarse_parts(self, planes, parts):
        row = self.row
        octet = self.octets()
        in_block = row < 8
        for p in planes:
            inside = 3 <= p <= 10
            tall = 16 if inside else 8
            ids = self.cells(LAYER, p, tall)
            lifted = ids > octet[0:tall]
            keep = in_block[0:tall]
            given = []
            if p >= 4:
                given.append((self.side_x(self.face_x, p - 1, tall), self.cells(LAYER, p - 1, tall), keep))
            if p <= 9:
                given.append((self.side_x(self.face_x, p, tall), self.cells(LAYER, p + 1, tall), keep))
            total = [jnp.zeros((tall, 256), F32) for _ in range(3)]
            if inside:
                face = read(self.face_y, p)
                given.append((face, roll(ids, -1, 0), (row < 7) | (row == 15)))
                given.append((roll(face, 1, 0), roll(ids, 1, 0), (row > 0) & (row < 9)))
                face = read(self.face_z, p)
                given.append((face, roll(ids, -1, 1), keep))
                given.append((roll(face, 1, 1), roll(ids, 1, 1), keep))
                own = read(self.rest, p)
                if p >= 4:
                    own = own + self.side_x(self.face_x, p - 1)
                if p <= 9:
                    own = own + self.side_x(self.face_x, p)
                total[1] = jnp.where(keep, own, 0.0)
            for face, beside, kept in given:
                face = jnp.where(kept, face, 0.0)
                step = beside - ids
                total[0] = total[0] - jnp.where(step == 1.0, face, 0.0)
                total[1] = total[1] - jnp.where(step == 0.0, face, 0.0)
                total[2] = total[2] - jnp.where(step == -1.0, face, 0.0)
            for oz in range(3):
                upper = jnp.where(lifted, total[oz], 0.0)
                ref, at = parts.at(p)
                ref[oz, 0, at, 0:tall] = total[oz] - upper
                ref[oz, 1, at, 0:tall] = upper

    def coarse_outer_faces(self, parts, outer_parts):
        row, octet = self.row, self.octets()
        for p, face in ((3, 2), (10, 10)):
            face = jnp.where(row < 8, self.side_x(self.face_x, face), 0.0)
            upper = jnp.where(self.cells(LAYER, p) > octet, face, 0.0)
            ref, at = parts.at(p)
            outer_parts[1, 0, p] = ref[1, 0, at] + (face - upper)
            outer_parts[1, 1, p] = ref[1, 1, at] + upper

    def octets(self):
        octet = (jnp.where(self.column < 192, self.column, self.column - 256) + 256) // BLOCK - 32
        return (octet + lax.axis_index("gz") * (128 // BLOCK)).astype(F32)

    def coarse_sums(self, planes, parts, sums, changed=None):
        for oz in range(3):
            for lift in range(2):
                for f in range(4):
                    groups = (planes,) if f < 2 else ([p for p in planes if p < 7], [p for p in planes if p >= 7])
                    for i, group in enumerate(groups):
                        top = bottom = None
                        for p in group:
                            part, spot = parts.at(p)
                            if changed is not None and oz == 1 and p in (3, 10):
                                part, spot = changed, p
                            value = part[oz, lift, spot, 0:8] * read(self.twice, p, f, 8)
                            top = value if top is None else top + value
                            if 3 <= p <= 10:
                                ref, at = self.twice.at(p)
                                value = part[oz, lift, spot, 8:16] * ref[f, at, 8:16]
                                bottom = value if bottom is None else bottom + value
                        ox = 1 if f < 2 else 2 * i
                        sums[oz, lift, ox, f & 1] = top + (roll(bottom, 4, 0) if f & 1 else bottom)


def store_slots(block, planes, smoothed):
    gx, gy = lax.axis_index("gx"), lax.axis_index("gy")
    rx_own, rx_low, rx_high = gx % 3, (gx + 2) % 3, (gx + 1) % 3
    ry_own, ry_low, ry_high = gy % 3, (gy + 2) % 3, (gy + 1) % 3
    sub = iota((8, 128), 0)
    zero = jnp.zeros((8, 128), F32)
    for i, x in enumerate(planes):
        ids = block.cells(LAYER, x + 3, 8)[:, 0:128]
        residue = ids - 3.0 * jnp.floor((ids + 0.5) * (1.0 / 3.0))
        rx_other, rx_none = (rx_low, rx_high) if x < 4 else (rx_high, rx_low)
        for ex, rx in ((0, rx_own), (1, rx_other)):
            own = read(block.twice, x + 3, 2 * ex, 8)[:, 0:128]
            other = read(block.twice, x + 3, 2 * ex + 1, 8)[:, 0:128]
            low = jnp.where(sub < 4, other, 0.0)
            high = other - low
            for rz in range(3):
                hit = jnp.abs(residue - rz) < 0.5
                smoothed[9 * rz + 3 * ry_own + rx, i] = jnp.where(hit, own, 0.0)
                smoothed[9 * rz + 3 * ry_low + rx, i] = jnp.where(hit, low, 0.0)
                smoothed[9 * rz + 3 * ry_high + rx, i] = jnp.where(hit, high, 0.0)
        for rz in range(3):
            for ry in range(3):
                smoothed[9 * rz + 3 * ry + rx_none, i] = zero


def inner_kernel(core, beside_z, beside_y, corner, *refs):
    arrays, (sums, parts_ref, held_once, held_twice, smoothed_hbm) = refs[:11], refs[11:16]
    smoothed, sem = refs[16:]
    ext = arrays[0]
    for f in ALL:
        for x in range(8):
            ext[f, x, 0:8, 0:128] = core[f, 8 * x : 8 * x + 8]
            ext[f, x, 8:16, 0:128] = beside_y[f, 8 * x : 8 * x + 8]
            ext[f, x, 0:8, 128:256] = unpacked(beside_z[f], x)
            ext[f, x, 8:16, 128:256] = unpacked(corner[f], x)
    block = Block(arrays, None)
    parts = Planes(parts_ref, None, 3)
    block.faces_x(range(3, 10))
    block.faces(range(3, 11))
    block.weights(range(4, 10))
    block.sweep(range(4, 10), block.ext, block.once)
    block.sweep(range(5, 9), block.once, block.twice)
    store_slots(block, (2, 3, 4, 5), smoothed)
    copy = pltpu.make_async_copy(smoothed, smoothed_hbm.at[:, 2:6], sem)
    copy.start()
    for held, source, first, last in ((held_once, block.ext, 3, 10), (held_twice, block.once, 4, 9)):
        for i, p in enumerate((first, last)):
            for f, total in enumerate(block.beside(p, source, low=i == 1, high=i == 0)):
                held[f, i] = total
    block.coarse_parts(range(3, 11), parts)
    block.coarse_sums(list(range(5, 9)), parts, sums)
    copy.wait()


def outer_kernel(from_one, from_other, *refs):
    arrays, (inner_sums, inner_parts, held_once, held_twice, _) = refs[:11], refs[11:16]
    smoothed_hbm, coarse = refs[16:18]
    outer = refs[18:29]
    outer_parts, sums, smoothed, sem = refs[29:]
    ext = outer[0]
    lane = iota((8, 128), 1)
    zero = jnp.zeros((8, 128), F32)

    def receive(pairs):
        for source, side in pairs:
            at = 0
            for d in range(3):
                plane = 11 + d if side else 2 - d
                for f in ALL:
                    into = f ^ 2 if f < 4 else f
                    if f in FIELDS_X[d]:
                        ext[into, plane, 0:8, 0:128] = source[at : at + 8]
                        at += 8
                    else:
                        ext[into, plane, 0:8, 0:128] = zero
            planes = (11, 12, 13) if side else (2, 1, 0)
            for f in ALL:
                for plane in planes:
                    ext[f, plane, 8:16, 0:128] = zero
            for d, row, f in ROWS_XY:
                into = f ^ 2 if f < 4 else f
                ext[into, planes[d], 8 + row : 9 + row, 0:128] = source[at : at + 1]
                at += 1
            at += 2
            for f in ALL:
                into = f ^ 2 if f < 4 else f
                first, last = 5 * f // 8, (5 * f + 4) // 8
                value = source[at + 8 * first : at + 8 * first + 8]
                if last > first:
                    value = jnp.where(lane >= 16 * (5 * f % 8), value, source[at + 8 * last : at + 8 * last + 8])
                value = roll(value, 48 * (1 - side) - 80 * f, 1)
                lateral = roll(value, -48 if side else 48, 1)
                for d in range(3):
                    slot = d if side else 7 - d
                    ext[into, planes[d], 0:8, 128:256] = unpacked(value, slot)
                    ext[into, planes[d], 8:16, 128:256] = unpacked(lateral, slot) if d < 2 else zero

    by_side("gx", from_one, from_other, receive)
    block = Block(arrays, outer)
    block.faces_x((0, 1, 2, 10, 11, 12))
    block.faces((1, 2, 11, 12))
    block.weights((1, 2, 3, 10, 11, 12))
    steps = (
        (held_once, block.ext, block.once, (1, 2, 11, 12), (3, 10)),
        (held_twice, block.once, block.twice, (2, 3, 10, 11), (4, 9)),
    )
    for held, source, target, whole, begun in steps:
        block.sweep(whole, source, target)
        for i, p in enumerate(begun):
            totals = block.beside_x(p, source, [held[f, i] for f in range(4)], low=i == 0, high=i == 1)
            block.relax(p, source, target, totals)
    store_slots(block, (0, 1, 6, 7), smoothed)
    copies = [
        pltpu.make_async_copy(smoothed.at[:, 0:2], smoothed_hbm.at[:, 0:2], sem.at[0]),
        pltpu.make_async_copy(smoothed.at[:, 2:4], smoothed_hbm.at[:, 6:8], sem.at[1]),
    ]
    for copy in copies:
        copy.start()

    parts = Planes(inner_parts, outer_parts, 3)
    block.coarse_parts((2, 11), parts)
    block.coarse_outer_faces(parts, outer_parts)
    block.coarse_sums([2, 3, 4, 9, 10, 11], parts, sums, outer_parts)
    spot = iota((16, 256), 1)
    place = (jnp.where(spot < 192, spot, spot - 256) + 256) // BLOCK - 32
    for oz in range(3):
        total = jnp.zeros((16, 16), F32)
        for lift in range(2):
            rows = []
            for oy in range(3):
                for ox in range(3):
                    ey = 0 if oy == 1 else 1
                    value = sums[oz, lift, ox, ey] + inner_sums[oz, lift, ox, ey]
                    if oy != 1:
                        value = value[0:4] if oy == 0 else value[4:8]
                    rows.append(jnp.sum(value, axis=0, keepdims=True))
            rows.append(jnp.zeros((7, 256), F32))
            chosen = (place + lift - (oz - 1) == iota((16, 256), 0)).astype(F32)
            total = total + lax.dot_general(
                chosen,
                jnp.concatenate(rows, axis=0),
                (((1,), (1,)), ((), ())),
                precision=lax.Precision.HIGHEST,
                preferred_element_type=F32,
            )
        coarse[:, 9 * oz : 9 * oz + 9] = total[:, 0:9] * (1.0 / (BLOCK * BLOCK))
    for copy in copies:
        copy.wait()


VMEM = pl.BlockSpec(memory_space=pltpu.VMEM)
HBM = pl.BlockSpec(memory_space=pltpu.HBM)


def call(kernel, outs, *operands, in_specs=None, out_specs=None, scratch=(), aliases=None, vmem=48 * 1024 * 1024):
    return pl.pallas_call(
        kernel,
        out_shape=[jax.ShapeDtypeStruct(shape, F32) for shape in outs],
        in_specs=in_specs or [VMEM] * len(operands),
        out_specs=out_specs or [VMEM] * len(outs),
        scratch_shapes=scratch,
        input_output_aliases=aliases or {},
        compiler_params=pltpu.CompilerParams(vmem_limit_bytes=vmem),
    )(*operands)


def exchange(axis, to_one, to_other):
    count = lax.axis_size(axis)
    one = [(i, ((i + 1) ^ 1) - 1) for i in range(1, count - 1)]
    other = [(i, i ^ 1) for i in range(count)]
    return lax.ppermute(to_one, axis, one), lax.ppermute(to_other, axis, other)


def per_device(basis, perm, storage, layer):
    block = (FIELDS, 64, 128)
    side = (FIELDS, 8, 128)
    core, edge = call(
        pack_kernel,
        (block, side),
        basis.reshape(27, 64, 128),
        perm.reshape(3, 64, 128),
        storage.reshape(64, 128),
        layer.reshape(64, 128),
        in_specs=[HBM] * 4,
        out_specs=[HBM, HBM],
        vmem=None,
        scratch=[
            pltpu.VMEM(block, F32),
            pltpu.VMEM(side, F32),
            pltpu.VMEM((27, 64, 128), F32),
            pltpu.VMEM((64, 128), jnp.int32),
            pltpu.SemaphoreType.DMA((7,)),
        ],
    )
    other, one = exchange("gz", edge, edge)
    (core,) = call(load_kernel, (block,), core)
    rows = (ROWS_Y + ROWS_Y // 8, 128)
    beside_z, to_one, to_other = call(y_kernel, (side, rows, rows), core, one, other)
    one, other = exchange("gy", to_one, to_other)
    rows = (ROWS_X + 96, 128)
    beside_y, corner, to_one, to_other = call(x_kernel, (block, side, rows, rows), core, beside_z, one, other)
    one, other = exchange("gx", to_one, to_other)

    def arrays(planes):
        return [
            (FIELDS, planes(3), 16, 256),
            (planes(3), 16, 256),
            (planes(3), 16, 256),
            (planes(3), 16, 256),
            (planes(3), 16, 256),
            (planes(3), 16, 256),
            (planes(3), 16, 256),
            (planes(3), 16, 256),
            (planes(4), 16, 256),
            (4, planes(4), 16, 256),
            (4, planes(5), 16, 256),
        ]

    sums = (3, 2, 3, 2, 8, 256)
    whole = (27, 8, 8, 128)
    half = pltpu.VMEM((27, 4, 8, 128), F32)
    held = (4, 2, 16, 256)
    outs = arrays(lambda first: 14 - 2 * first) + [sums, (3, 2, 8, 16, 256), held, held, whole]
    inner = call(
        inner_kernel,
        outs,
        core,
        beside_z,
        beside_y,
        corner,
        out_specs=[VMEM] * 15 + [HBM],
        scratch=[half, pltpu.SemaphoreType.DMA],
    )
    smoothed, coarse = call(
        outer_kernel,
        (whole, (16, 27)),
        one,
        other,
        *inner,
        in_specs=[VMEM] * 17 + [HBM],
        out_specs=[HBM, VMEM],
        scratch=[pltpu.VMEM(shape, F32) for shape in arrays(lambda first: 14)]
        + [pltpu.VMEM((3, 2, 14, 16, 256), F32), pltpu.VMEM(sums, F32), half, pltpu.SemaphoreType.DMA((2,))],
        aliases={17: 0},
    )
    return smoothed, coarse.T.reshape(27, 1, 1, 16)


def solution(mesh):
    return jax.shard_map(
        per_device,
        mesh=mesh,
        in_specs=(
            P(None, "gx", "gy", "gz"),
            P(None, "gx", "gy", "gz"),
            P("gx", "gy", "gz"),
            P("gx", "gy", "gz"),
        ),
        out_specs=(P(None, "gx", "gy", "gz"), P(None, "gx", "gy", "gz")),
        check_vma=False,
    )
```

```python
import functools

import jax
import jax.numpy as jnp
from jax import lax
from jax.experimental import pallas as pl
from jax.experimental.pallas import tpu as pltpu
from jax.sharding import PartitionSpec as P

BLOCK = 8
FIELDS = 9
PX, PY, PZ, STORAGE, LAYER = 4, 5, 6, 7, 8
ALL = tuple(range(FIELDS))
FIELDS_X = (ALL, ALL, (0, 1, 2, 3, PX, LAYER))
FIELDS_Y = (ALL, ALL, (0, 1, 2, 3, PY, LAYER))
ROWS_Y = 8 * sum(len(f) for f in FIELDS_Y)
ROWS_X = 8 * sum(len(f) for f in FIELDS_X)
FIELDS_XY = (0, 1, 2, 3, PX, PY, LAYER)
ROWS_XY = (
    [(0, row, f) for row in (7, 0) for f in ALL]
    + [(0, row, f) for row in (6, 1) for f in FIELDS_XY]
    + [(1, row, f) for row in (7, 0) for f in FIELDS_XY]
)
F32 = jnp.float32


def iota(shape, dim):
    return lax.broadcasted_iota(jnp.int32, shape, dim)


def roll(value, shift, axis):
    return pltpu.roll(value, shift % value.shape[axis], axis)


def pack_kernel(basis_hbm, perm_hbm, storage_hbm, layer_hbm, core_hbm, edge_hbm, core, edge, basis, layer, sems):
    rest = [
        pltpu.make_async_copy(layer_hbm, layer, sems.at[0]),
        pltpu.make_async_copy(perm_hbm, core.at[PX : PZ + 1], sems.at[1]),
        pltpu.make_async_copy(storage_hbm, core.at[STORAGE], sems.at[2]),
    ]
    arriving = pltpu.make_async_copy(basis_hbm, basis, sems.at[3])
    for copy in rest + [arriving]:
        copy.start()
    gx, gy = lax.axis_index("gx"), lax.axis_index("gy")
    nx, ny = lax.axis_size("gx"), lax.axis_size("gy")
    sub, lane = iota((8, 128), 0), iota((8, 128), 1)
    rx_own, rx_low, rx_high = gx % 3, (gx + 2) % 3, (gx + 1) % 3
    ry_own, ry_low, ry_high = gy % 3, (gy + 2) % 3, (gy + 1) % 3
    low_rows = sub < 4
    y_valid = jnp.where(low_rows, (gy > 0).astype(F32), (gy < ny - 1).astype(F32))

    def moved(value, x):
        return roll(jnp.where(lane < 4, value, roll(value, 16, 1)), 16 * x, 1)

    for copy in rest:
        copy.wait()
    ids = layer[...].astype(F32)
    core[LAYER] = ids
    kept = [pltpu.make_async_copy(core.at[4:9], core_hbm.at[4:9], sems.at[4])]
    kept[0].start()
    residue = ids - 3.0 * jnp.floor((ids + 0.5) * (1.0 / 3.0))
    strip = lane // 16
    for f in range(4, FIELDS):
        packed = jnp.zeros((8, 128), F32)
        for x in range(8):
            packed = jnp.where(strip == x, moved(core[f, 8 * x : 8 * x + 8], x), packed)
        edge[f] = packed

    packed = [jnp.zeros((8, 128), F32) for _ in range(4)]
    arriving.wait()
    for x in range(8):
        here = residue[8 * x : 8 * x + 8]
        is_zero, is_one = here < 0.5, here < 1.5

        def at(rx, ry):
            first, second, third = (basis[9 * rz + 3 * ry + rx, 8 * x : 8 * x + 8] for rz in range(3))
            return jnp.where(is_zero, first, jnp.where(is_one, second, third))

        rx_other = rx_low if x < 4 else rx_high
        x_valid = ((gx > 0) if x < 4 else (gx < nx - 1)).astype(F32)
        for ex, rx in enumerate((rx_own, rx_other)):
            own = at(rx, ry_own)
            other = jnp.where(low_rows, at(rx, ry_low), at(rx, ry_high)) * y_valid
            if ex:
                own, other = own * x_valid, other * x_valid
            for f, value in ((2 * ex, own), (2 * ex + 1, other)):
                core[f, 8 * x : 8 * x + 8] = value
                packed[f] = jnp.where(strip == x, moved(value, x), packed[f])
    for f in range(4):
        edge[f] = packed[f]
    kept.append(pltpu.make_async_copy(edge, edge_hbm, sems.at[5]))
    kept.append(pltpu.make_async_copy(core.at[0:4], core_hbm.at[0:4], sems.at[6]))
    kept[1].start()
    kept[2].start()
    for copy in kept:
        copy.wait()


def load_kernel(core_hbm, core):
    core[...] = core_hbm[...]


def by_side(axis, one, other, body):
    even = lax.axis_index(axis) % 2 == 0
    pl.when(even)(lambda: body(((one, 0), (other, 1))))
    pl.when(jnp.logical_not(even))(lambda: body(((one, 1), (other, 0))))


def y_kernel(core, from_one, from_other, beside_z, to_one, to_other):
    lane = iota((8, 128), 1)
    high = (lane % 16 < 4).astype(jnp.int32)
    odd = lax.axis_index("gz") % 2
    for f in ALL:
        beside_z[f] = jnp.where(high != odd, from_one[f], from_other[f])

    def send(pairs):
        for out, side in pairs:
            at = 0
            for d, fields in enumerate(FIELDS_Y):
                y = 7 - d if side else d
                for f in fields:
                    out[at : at + 8] = core[f, pl.ds(y, 8, stride=8), :]
                    at += 8
            for d, fields in enumerate(FIELDS_Y):
                y = 7 - d if side else d
                for f in fields:
                    out[at : at + 1] = beside_z[f, y : y + 1]
                    at += 1

    by_side("gy", to_one, to_other, send)


def x_kernel(core, beside_z, from_one, from_other, beside_y, corner, to_one, to_other):
    lane = iota((8, 128), 1)
    zero = jnp.zeros((8, 128), F32)
    beside_y[...] = jnp.zeros(beside_y.shape, F32)
    corner[...] = jnp.zeros(corner.shape, F32)

    def receive(pairs):
        for source, side in pairs:
            at = 0
            for d, fields in enumerate(FIELDS_Y):
                row = d if side else 7 - d
                for f in fields:
                    into = f ^ 1 if f < 4 else f
                    beside_y[into, pl.ds(row, 8, stride=8), :] = source[at : at + 8]
                    at += 8
            for d, fields in enumerate(FIELDS_Y):
                row = d if side else 7 - d
                for f in fields:
                    into = f ^ 1 if f < 4 else f
                    corner[into, row : row + 1] = source[at : at + 1]
                    at += 1

    by_side("gy", from_one, from_other, receive)

    def send(pairs):
        for out, side in pairs:
            at = 0
            for d, fields in enumerate(FIELDS_X):
                x = 7 - d if side else d
                for f in fields:
                    out[at : at + 8] = core[f, 8 * x : 8 * x + 8]
                    at += 8
            for d, row, f in ROWS_XY:
                from_row = 8 * (7 - d if side else d) + row
                out[at : at + 1] = beside_y[f, from_row : from_row + 1]
                at += 1
            out[at : at + 2] = jnp.zeros((2, 128), F32)
            at += 2
            strips = []
            for f in ALL:
                value = jnp.where((lane >= 48) & (lane < 80), roll(corner[f], -48 if side else 48, 1), beside_z[f])
                strips.append(roll(value, 80 * f - 48 * side, 1))
            for v in range(6):
                value = zero
                for f in ALL:
                    start, stop = max(5 * f, 8 * v), min(5 * f + 5, 8 * v + 8)
                    if start < stop:
                        inside = (lane >= 16 * (start - 8 * v)) & (lane < 16 * (stop - 8 * v))
                        value = jnp.where(inside, strips[f], value)
                out[at : at + 8] = value
                at += 8

    by_side("gx", to_one, to_other, send)


def harmonic(first, second):
    total = first + second
    return 2.0 * first * second / jnp.where(total > 0.0, total, 1.0)


def unpacked(value, slot):
    lane = iota((8, 128), 1)
    value = roll(value, -16 * slot, 1)
    return jnp.where(lane < 3, value, jnp.where(lane >= 117, roll(value, 112, 1), 0.0))


class Planes:
    def __init__(self, inner, outer, first):
        self.inner, self.outer, self.first, self.last = inner, outer, first, 13 - first

    def at(self, p, shift=0):
        if self.first <= p <= self.last - shift:
            return self.inner, p - self.first
        return self.outer, p


def read(planes, p, f=None, tall=16, shift=0):
    ref, p = planes.at(p, shift)
    return ref[p, 0:tall] if f is None else ref[f, p, 0:tall]


def write(planes, value, p, f=None, shift=0):
    ref, p = planes.at(p, shift)
    rows = value.shape[0]
    if f is None:
        ref[p, 0:rows] = value
    else:
        ref[f, p, 0:rows] = value


class Block:
    def __init__(self, inner, outer):
        names = ("ext", "face_x", "near_x", "face_y", "face_z", "near_y", "near_z", "rest", "weight", "once", "twice")
        first = (3, 3, 3, 3, 3, 3, 3, 3, 4, 4, 5)
        for i, name in enumerate(names):
            setattr(self, name, Planes(inner[i], outer[i] if outer else None, first[i]))
        self.row, self.column = iota((16, 256), 0), iota((16, 256), 1)

    def cells(self, f, p, tall=16):
        return read(self.ext, p, f, tall)

    def side_x(self, planes, p, tall=16):
        return read(planes, p, None, tall, 1)

    def faces_x(self, planes):
        for p in planes:
            face = harmonic(self.cells(PX, p), self.cells(PX, p + 1))
            write(self.face_x, face, p, None, 1)
            write(self.near_x, jnp.where(self.cells(LAYER, p) == self.cells(LAYER, p + 1), face, 0.0), p, None, 1)

    def faces(self, planes):
        for p in planes:
            ids = self.cells(LAYER, p)
            total = self.cells(STORAGE, p)
            for f, axis, face_at, near_at in ((PY, 0, self.face_y, self.near_y), (PZ, 1, self.face_z, self.near_z)):
                across = self.cells(f, p)
                face = harmonic(across, roll(across, -1, axis))
                write(face_at, face, p)
                write(near_at, jnp.where(ids == roll(ids, -1, axis), face, 0.0), p)
                total = total + (face + roll(face, 1, axis))
            write(self.rest, total, p)

    def diagonal(self, p):
        return read(self.rest, p) + (self.side_x(self.face_x, p - 1) + self.side_x(self.face_x, p))

    def weights(self, planes):
        for p in planes:
            total = self.diagonal(p)
            write(self.weight, (2.0 / 3.0) / jnp.where(total > 0.0, total, 1.0), p)

    def height(self, p, source):
        return 8 if p in ((1, 12) if source is self.ext else (2, 11)) else 16

    def beside(self, p, source, low=True, high=True):
        tall = self.height(p, source)
        near_y, near_z = read(self.near_y, p), read(self.near_z, p, None, tall)
        near_y_other = jnp.where(self.row == 3, 0.0, near_y)
        totals = []
        for f in range(4):
            whole = read(source, p, f)
            own = whole[0:tall]
            side = near_y_other if f & 1 else near_y
            total = side[0:tall] * roll(whole, -1, 0)[0:tall] + roll(side * whole, 1, 0)[0:tall]
            totals.append(total + (near_z * roll(own, -1, 1) + roll(near_z * own, 1, 1)))
        return self.beside_x(p, source, totals, low, high)

    def beside_x(self, p, source, totals, low=False, high=False):
        tall = self.height(p, source)
        totals = list(totals)
        if low:
            face = self.side_x(self.near_x, p - 1, tall)
            for f in range(2 if p == 7 else 4):
                totals[f] = totals[f] + face * read(source, p - 1, f, tall)
        if high:
            face = self.side_x(self.near_x, p, tall)
            for f in range(2 if p == 6 else 4):
                totals[f] = totals[f] + face * read(source, p + 1, f, tall)
        return totals

    def relax(self, p, source, target, totals):
        gx, gy = lax.axis_index("gx"), lax.axis_index("gy")
        nx, ny = lax.axis_size("gx"), lax.axis_size("gy")
        tall = self.height(p, source)
        row = self.row[0:tall]
        y_valid = jnp.where((row < 4) | (row >= 12), (gy > 0).astype(F32), (gy < ny - 1).astype(F32))
        x_valid = ((gx > 0) if p < 7 else (gx < nx - 1)).astype(F32)
        scale = read(self.weight, p, None, tall)
        scale_other = scale * y_valid
        updated = []
        for f in range(4):
            factor = scale_other if f & 1 else scale
            if f & 2:
                factor = factor * x_valid
            updated.append(read(source, p, f, tall) * (1.0 / 3.0) + factor * totals[f])
        total = (updated[0] + updated[1]) + (updated[2] + updated[3])
        inverse = 1.0 / jnp.where(total > 0.0, total, 1.0)
        for f in range(4):
            write(target, updated[f] * inverse, p, f)

    def sweep(self, planes, source, target):
        for p in planes:
            self.relax(p, source, target, self.beside(p, source))

    def coarse_parts(self, planes, parts):
        row = self.row
        octet = self.octets()
        above, below = (row < 7) | (row == 15), (row > 0) & (row < 9)
        for p in planes:
            inside = 3 <= p <= 10
            ids = self.cells(LAYER, p)
            up, own, down = (jnp.zeros((8, 256), F32) for _ in range(3))
            given = []
            if p >= 4:
                given.append((self.side_x(self.face_x, p - 1, 8), self.side_x(self.near_x, p - 1, 8), self.cells(LAYER, p - 1, 8)))
            if p <= 9:
                given.append((self.side_x(self.face_x, p, 8), self.side_x(self.near_x, p, 8), self.cells(LAYER, p + 1, 8)))
            if inside:
                own = read(self.rest, p, None, 8)
                for face, _, _ in given:
                    own = own + face
                face, near, top = read(self.face_z, p, None, 8), read(self.near_z, p, None, 8), ids[0:8]
                given.append((face, near, roll(top, -1, 1)))
                given.append((roll(face, 1, 1), roll(near, 1, 1), roll(top, 1, 1)))
            for face, near, beside in given:
                apart = face - near
                higher = jnp.where(beside > ids[0:8], apart, 0.0)
                up, own, down = up - higher, own - near, down - (apart - higher)
            total = [up, own, down]
            if inside:
                up, own, down = (jnp.zeros((16, 256), F32) for _ in range(3))
                face, near = read(self.face_y, p), read(self.near_y, p)
                for shift, keep in ((0, above), (1, below)):
                    apart, close = face - near, near
                    beside = roll(ids, 1 if shift else -1, 0)
                    if shift:
                        apart, close = roll(apart, 1, 0), roll(close, 1, 0)
                    apart, close = jnp.where(keep, apart, 0.0), jnp.where(keep, close, 0.0)
                    higher = jnp.where(beside > ids, apart, 0.0)
                    up, own, down = up - higher, own - close, down - (apart - higher)
                total = [jnp.concatenate([t + y[0:8], y[8:16]], axis=0) for t, y in zip(total, (up, own, down))]
            tall = 16 if inside else 8
            lifted = ids[0:tall] > octet[0:tall]
            for oz in range(3):
                upper = jnp.where(lifted, total[oz], 0.0)
                ref, at = parts.at(p)
                ref[oz, 0, at, 0:tall] = total[oz] - upper
                ref[oz, 1, at, 0:tall] = upper

    def coarse_outer_face(self, p, face, parts, outer_parts):
        face = jnp.where(self.row < 8, self.side_x(self.face_x, face), 0.0)
        upper = jnp.where(self.cells(LAYER, p) > self.octets(), face, 0.0)
        ref, at = parts.at(p)
        outer_parts[1, 0, p] = ref[1, 0, at] + (face - upper)
        outer_parts[1, 1, p] = ref[1, 1, at] + upper

    def octets(self):
        octet = (jnp.where(self.column < 192, self.column, self.column - 256) + 256) // BLOCK - 32
        return (octet + lax.axis_index("gz") * (128 // BLOCK)).astype(F32)

    def coarse_sums(self, planes, parts, sums, changed=None):
        for oz in range(3):
            for lift in range(2):
                for f in range(4):
                    groups = (planes,) if f < 2 else ([p for p in planes if p < 7], [p for p in planes if p >= 7])
                    for i, group in enumerate(groups):
                        if not group:
                            continue
                        top = bottom = None
                        for p in group:
                            part, spot = parts.at(p)
                            if changed is not None and oz == 1 and p in (3, 10):
                                part, spot = changed, p
                            value = part[oz, lift, spot, 0:8] * read(self.twice, p, f, 8)
                            top = value if top is None else top + value
                            if 3 <= p <= 10:
                                ref, at = self.twice.at(p)
                                value = part[oz, lift, spot, 8:16] * ref[f, at, 8:16]
                                bottom = value if bottom is None else bottom + value
                        ox = 1 if f < 2 else 2 * i
                        sums[oz, lift, ox, f & 1] = top + (roll(bottom, 4, 0) if f & 1 else bottom)


def store_slots(block, planes, smoothed):
    gx, gy = lax.axis_index("gx"), lax.axis_index("gy")
    rx_own, rx_low, rx_high = gx % 3, (gx + 2) % 3, (gx + 1) % 3
    ry_own, ry_low, ry_high = gy % 3, (gy + 2) % 3, (gy + 1) % 3
    sub = iota((8, 128), 0)
    zero = jnp.zeros((8, 128), F32)
    for i, x in enumerate(planes):
        ids = block.cells(LAYER, x + 3, 8)[:, 0:128]
        residue = ids - 3.0 * jnp.floor((ids + 0.5) * (1.0 / 3.0))
        rx_other, rx_none = (rx_low, rx_high) if x < 4 else (rx_high, rx_low)
        for ex, rx in ((0, rx_own), (1, rx_other)):
            own = read(block.twice, x + 3, 2 * ex, 8)[:, 0:128]
            other = read(block.twice, x + 3, 2 * ex + 1, 8)[:, 0:128]
            low = jnp.where(sub < 4, other, 0.0)
            high = other - low
            for rz in range(3):
                hit = jnp.abs(residue - rz) < 0.5
                smoothed[9 * rz + 3 * ry_own + rx, i] = jnp.where(hit, own, 0.0)
                smoothed[9 * rz + 3 * ry_low + rx, i] = jnp.where(hit, low, 0.0)
                smoothed[9 * rz + 3 * ry_high + rx, i] = jnp.where(hit, high, 0.0)
        for rz in range(3):
            for ry in range(3):
                smoothed[9 * rz + 3 * ry + rx_none, i] = zero


def inner_kernel(core, beside_z, beside_y, corner, *refs):
    arrays, (sums, parts_ref, held_once, held_twice, smoothed_hbm) = refs[:11], refs[11:16]
    smoothed, sem = refs[16:]
    ext = arrays[0]
    for f in ALL:
        for x in range(8):
            ext[f, x, 0:8, 0:128] = core[f, 8 * x : 8 * x + 8]
            ext[f, x, 8:16, 0:128] = beside_y[f, 8 * x : 8 * x + 8]
            ext[f, x, 0:8, 128:256] = unpacked(beside_z[f], x)
            ext[f, x, 8:16, 128:256] = unpacked(corner[f], x)
    block = Block(arrays, None)
    parts = Planes(parts_ref, None, 3)
    block.faces_x(range(3, 10))
    block.faces(range(3, 11))
    block.weights(range(4, 10))
    block.sweep(range(4, 10), block.ext, block.once)
    block.sweep(range(5, 9), block.once, block.twice)
    store_slots(block, (2, 3, 4, 5), smoothed)
    copy = pltpu.make_async_copy(smoothed, smoothed_hbm.at[:, 2:6], sem)
    copy.start()
    for held, source, first, last in ((held_once, block.ext, 3, 10), (held_twice, block.once, 4, 9)):
        for i, p in enumerate((first, last)):
            for f, total in enumerate(block.beside(p, source, low=i == 1, high=i == 0)):
                held[f, i] = total
    block.coarse_parts(range(3, 11), parts)
    block.coarse_sums(list(range(5, 9)), parts, sums)
    copy.wait()


def receive_planes(source, side, ext):
    lane = iota((8, 128), 1)
    zero = jnp.zeros((8, 128), F32)
    planes = (11, 12, 13) if side else (2, 1, 0)
    at = 0
    for d in range(3):
        for f in ALL:
            into = f ^ 2 if f < 4 else f
            if f in FIELDS_X[d]:
                ext[into, planes[d], 0:8, 0:128] = source[at : at + 8]
                at += 8
            else:
                ext[into, planes[d], 0:8, 0:128] = zero
            ext[into, planes[d], 8:16, 0:128] = zero
    for d, row, f in ROWS_XY:
        into = f ^ 2 if f < 4 else f
        ext[into, planes[d], 8 + row : 9 + row, 0:128] = source[at : at + 1]
        at += 1
    at += 2
    for f in ALL:
        into = f ^ 2 if f < 4 else f
        first, last = 5 * f // 8, (5 * f + 4) // 8
        value = source[at + 8 * first : at + 8 * first + 8]
        if last > first:
            value = jnp.where(lane >= 16 * (5 * f % 8), value, source[at + 8 * last : at + 8 * last + 8])
        value = roll(value, 48 * (1 - side) - 80 * f, 1)
        lateral = roll(value, -48 if side else 48, 1)
        for d in range(3):
            slot = d if side else 7 - d
            ext[into, planes[d], 0:8, 128:256] = unpacked(value, slot)
            ext[into, planes[d], 8:16, 128:256] = unpacked(lateral, slot) if d < 2 else zero


def outer_kernel(last, source, *refs):
    arrays, (inner_sums, inner_parts, held_once, held_twice, _), refs = refs[:11], refs[11:16], refs[16:]
    if last:
        (first_sums, smoothed_hbm, coarse), refs = refs[:3], refs[3:]
    else:
        (smoothed_hbm, sums), refs = refs[:2], refs[2:]
    outer, refs = refs[:11], refs[11:]
    outer_parts, smoothed, sem = refs[:3]
    if last:
        sums = refs[3]
    block = Block(arrays, outer)
    parts = Planes(inner_parts, outer_parts, 3)
    even = lax.axis_index("gx") % 2 == 0
    high = even if last else jnp.logical_not(even)
    copy = pltpu.make_async_copy(smoothed, smoothed_hbm.at[:, pl.ds(jnp.where(high, 6, 0), 2)], sem)
    sums[...] = jnp.zeros(sums.shape, F32)

    def add(side):
        def plane(d):
            return 10 + d if side else 3 - d

        def face(d):
            return 9 + d if side else 3 - d

        receive_planes(source, side, outer[0])
        block.faces_x([face(d) for d in (1, 2, 3)])
        block.faces([plane(1), plane(2)])
        block.weights([plane(0), plane(1), plane(2)])
        steps = (
            (held_once, block.ext, block.once, (2, 1), 0),
            (held_twice, block.once, block.twice, (1, 0), -1),
        )
        for held, values, target, whole, begun in steps:
            block.sweep([plane(d) for d in whole], values, target)
            p = plane(begun)
            totals = [held[f, side] for f in range(4)]
            totals = block.beside_x(p, values, totals, low=not side, high=bool(side))
            block.relax(p, values, target, totals)
        store_slots(block, (6, 7) if side else (0, 1), smoothed)
        copy.start()
        block.coarse_parts([plane(1)], parts)
        block.coarse_outer_face(plane(0), face(1), parts, outer_parts)
        block.coarse_sums(sorted(plane(d) for d in (-1, 0, 1)), parts, sums, outer_parts)

    pl.when(high)(lambda: add(1))
    pl.when(jnp.logical_not(high))(lambda: add(0))
    if last:
        spot = iota((16, 256), 1)
        place = (jnp.where(spot < 192, spot, spot - 256) + 256) // BLOCK - 32
        for oz in range(3):
            total = jnp.zeros((16, 16), F32)
            for lift in range(2):
                rows = []
                for oy in range(3):
                    for ox in range(3):
                        ey = 0 if oy == 1 else 1
                        value = inner_sums[oz, lift, ox, ey] + first_sums[oz, lift, ox, ey] + sums[oz, lift, ox, ey]
                        if oy != 1:
                            value = value[0:4] if oy == 0 else value[4:8]
                        rows.append(jnp.sum(value, axis=0, keepdims=True))
                rows.append(jnp.zeros((7, 256), F32))
                chosen = (place + lift - (oz - 1) == iota((16, 256), 0)).astype(F32)
                total = total + lax.dot_general(
                    chosen,
                    jnp.concatenate(rows, axis=0),
                    (((1,), (1,)), ((), ())),
                    precision=lax.Precision.HIGHEST,
                    preferred_element_type=F32,
                )
            coarse[:, 9 * oz : 9 * oz + 9] = total[:, 0:9] * (1.0 / (BLOCK * BLOCK))
    copy.wait()


VMEM = pl.BlockSpec(memory_space=pltpu.VMEM)
HBM = pl.BlockSpec(memory_space=pltpu.HBM)


def call(kernel, outs, *operands, in_specs=None, out_specs=None, scratch=(), aliases=None, vmem=48 * 1024 * 1024):
    return pl.pallas_call(
        kernel,
        out_shape=[jax.ShapeDtypeStruct(shape, F32) for shape in outs],
        in_specs=in_specs or [VMEM] * len(operands),
        out_specs=out_specs or [VMEM] * len(outs),
        scratch_shapes=scratch,
        input_output_aliases=aliases or {},
        compiler_params=pltpu.CompilerParams(vmem_limit_bytes=vmem),
    )(*operands)


def exchange(axis, to_one, to_other):
    count = lax.axis_size(axis)
    one = [(i, ((i + 1) ^ 1) - 1) for i in range(1, count - 1)]
    other = [(i, i ^ 1) for i in range(count)]
    return lax.ppermute(to_one, axis, one), lax.ppermute(to_other, axis, other)


def per_device(basis, perm, storage, layer):
    block = (FIELDS, 64, 128)
    side = (FIELDS, 8, 128)
    core, edge = call(
        pack_kernel,
        (block, side),
        basis.reshape(27, 64, 128),
        perm.reshape(3, 64, 128),
        storage.reshape(64, 128),
        layer.reshape(64, 128),
        in_specs=[HBM] * 4,
        out_specs=[HBM, HBM],
        vmem=None,
        scratch=[
            pltpu.VMEM(block, F32),
            pltpu.VMEM(side, F32),
            pltpu.VMEM((27, 64, 128), F32),
            pltpu.VMEM((64, 128), jnp.int32),
            pltpu.SemaphoreType.DMA((7,)),
        ],
    )
    other, one = exchange("gz", edge, edge)
    (core,) = call(load_kernel, (block,), core)
    rows = (ROWS_Y + ROWS_Y // 8, 128)
    beside_z, to_one, to_other = call(y_kernel, (side, rows, rows), core, one, other)
    one, other = exchange("gy", to_one, to_other)
    rows = (ROWS_X + 96, 128)
    beside_y, corner, to_one, to_other = call(x_kernel, (block, side, rows, rows), core, beside_z, one, other)
    one, other = exchange("gx", to_one, to_other)

    def arrays(planes):
        return [
            (FIELDS, planes(3), 16, 256),
            (planes(3), 16, 256),
            (planes(3), 16, 256),
            (planes(3), 16, 256),
            (planes(3), 16, 256),
            (planes(3), 16, 256),
            (planes(3), 16, 256),
            (planes(3), 16, 256),
            (planes(4), 16, 256),
            (4, planes(4), 16, 256),
            (4, planes(5), 16, 256),
        ]

    sums = (3, 2, 3, 2, 8, 256)
    whole = (27, 8, 8, 128)
    half = pltpu.VMEM((27, 4, 8, 128), F32)
    held = (4, 2, 16, 256)
    outs = arrays(lambda first: 14 - 2 * first) + [sums, (3, 2, 8, 16, 256), held, held, whole]
    inner = call(
        inner_kernel,
        outs,
        core,
        beside_z,
        beside_y,
        corner,
        out_specs=[VMEM] * 15 + [HBM],
        scratch=[half, pltpu.SemaphoreType.DMA],
    )
    scratch = [pltpu.VMEM(shape, F32) for shape in arrays(lambda first: 14)]
    scratch += [pltpu.VMEM((3, 2, 14, 16, 256), F32), pltpu.VMEM((27, 2, 8, 128), F32), pltpu.SemaphoreType.DMA]
    smoothed, first_sums = call(
        functools.partial(outer_kernel, False),
        (whole, sums),
        one,
        *inner,
        in_specs=[VMEM] * 16 + [HBM],
        out_specs=[HBM, VMEM],
        scratch=scratch,
        aliases={16: 0},
    )
    smoothed, coarse = call(
        functools.partial(outer_kernel, True),
        (whole, (16, 27)),
        other,
        *inner[:-1],
        smoothed,
        first_sums,
        in_specs=[VMEM] * 16 + [HBM, VMEM],
        out_specs=[HBM, VMEM],
        scratch=scratch + [pltpu.VMEM(sums, F32)],
        aliases={16: 0},
    )
    return smoothed, coarse.T.reshape(27, 1, 1, 16)


def solution(mesh):
    return jax.shard_map(
        per_device,
        mesh=mesh,
        in_specs=(
            P(None, "gx", "gy", "gz"),
            P(None, "gx", "gy", "gz"),
            P("gx", "gy", "gz"),
            P("gx", "gy", "gz"),
        ),
        out_specs=(P(None, "gx", "gy", "gz"), P(None, "gx", "gy", "gz")),
        check_vma=False,
    )
```

```python
import functools

import jax
import jax.numpy as jnp
from jax import lax
from jax.experimental import pallas as pl
from jax.experimental.pallas import tpu as pltpu
from jax.sharding import PartitionSpec as P

BLOCK = 8
FIELDS = 9
PX, PY, PZ, STORAGE, LAYER = 4, 5, 6, 7, 8
ALL = tuple(range(FIELDS))
FIELDS_X = (ALL, ALL, (0, 1, 2, 3, PX, LAYER))
FIELDS_Y = (ALL, ALL, (0, 1, 2, 3, PY, LAYER))
ROWS_Y = 8 * sum(len(f) for f in FIELDS_Y)
ROWS_X = 8 * sum(len(f) for f in FIELDS_X)
FIELDS_XY = (0, 1, 2, 3, PX, PY, LAYER)
ROWS_XY = (
    [(0, row, f) for row in (7, 0) for f in ALL]
    + [(0, row, f) for row in (6, 1) for f in FIELDS_XY]
    + [(1, row, f) for row in (7, 0) for f in FIELDS_XY]
)
F32 = jnp.float32


def iota(shape, dim):
    return lax.broadcasted_iota(jnp.int32, shape, dim)


def roll(value, shift, axis):
    return pltpu.roll(value, shift % value.shape[axis], axis)


def pack_kernel(basis_hbm, perm_hbm, storage_hbm, layer_hbm, core_hbm, edge_hbm, core, edge, basis, layer, sems):
    rest = [
        pltpu.make_async_copy(layer_hbm, layer, sems.at[0]),
        pltpu.make_async_copy(perm_hbm, core.at[PX : PZ + 1], sems.at[1]),
        pltpu.make_async_copy(storage_hbm, core.at[STORAGE], sems.at[2]),
    ]
    arriving = pltpu.make_async_copy(basis_hbm, basis, sems.at[3])
    for copy in rest + [arriving]:
        copy.start()
    gx, gy = lax.axis_index("gx"), lax.axis_index("gy")
    nx, ny = lax.axis_size("gx"), lax.axis_size("gy")
    sub, lane = iota((8, 128), 0), iota((8, 128), 1)
    rx_own, rx_low, rx_high = gx % 3, (gx + 2) % 3, (gx + 1) % 3
    ry_own, ry_low, ry_high = gy % 3, (gy + 2) % 3, (gy + 1) % 3
    low_rows = sub < 4
    y_valid = jnp.where(low_rows, (gy > 0).astype(F32), (gy < ny - 1).astype(F32))

    def moved(value, x):
        return roll(jnp.where(lane < 4, value, roll(value, 16, 1)), 16 * x, 1)

    for copy in rest:
        copy.wait()
    ids = layer[...].astype(F32)
    core[LAYER] = ids
    kept = [pltpu.make_async_copy(core.at[4:9], core_hbm.at[4:9], sems.at[4])]
    kept[0].start()
    residue = ids - 3.0 * jnp.floor((ids + 0.5) * (1.0 / 3.0))
    strip = lane // 16
    for f in range(4, FIELDS):
        packed = jnp.zeros((8, 128), F32)
        for x in range(8):
            packed = jnp.where(strip == x, moved(core[f, 8 * x : 8 * x + 8], x), packed)
        edge[f] = packed

    packed = [jnp.zeros((8, 128), F32) for _ in range(4)]
    arriving.wait()
    for x in range(8):
        here = residue[8 * x : 8 * x + 8]
        is_zero, is_one = here < 0.5, here < 1.5

        def at(rx, ry):
            first, second, third = (basis[9 * rz + 3 * ry + rx, 8 * x : 8 * x + 8] for rz in range(3))
            return jnp.where(is_zero, first, jnp.where(is_one, second, third))

        rx_other = rx_low if x < 4 else rx_high
        x_valid = ((gx > 0) if x < 4 else (gx < nx - 1)).astype(F32)
        for ex, rx in enumerate((rx_own, rx_other)):
            own = at(rx, ry_own)
            other = jnp.where(low_rows, at(rx, ry_low), at(rx, ry_high)) * y_valid
            if ex:
                own, other = own * x_valid, other * x_valid
            for f, value in ((2 * ex, own), (2 * ex + 1, other)):
                core[f, 8 * x : 8 * x + 8] = value
                packed[f] = jnp.where(strip == x, moved(value, x), packed[f])
    for f in range(4):
        edge[f] = packed[f]
    kept.append(pltpu.make_async_copy(edge, edge_hbm, sems.at[5]))
    kept.append(pltpu.make_async_copy(core.at[0:4], core_hbm.at[0:4], sems.at[6]))
    kept[1].start()
    kept[2].start()
    for copy in kept:
        copy.wait()


def load_kernel(core_hbm, core):
    core[...] = core_hbm[...]


def by_side(axis, one, other, body):
    even = lax.axis_index(axis) % 2 == 0
    pl.when(even)(lambda: body(((one, 0), (other, 1))))
    pl.when(jnp.logical_not(even))(lambda: body(((one, 1), (other, 0))))


def y_kernel(core, from_one, from_other, beside_z, to_one, to_other):
    lane = iota((8, 128), 1)
    high = (lane % 16 < 4).astype(jnp.int32)
    odd = lax.axis_index("gz") % 2
    for f in ALL:
        beside_z[f] = jnp.where(high != odd, from_one[f], from_other[f])

    def send(pairs):
        for out, side in pairs:
            at = 0
            for d, fields in enumerate(FIELDS_Y):
                y = 7 - d if side else d
                for f in fields:
                    out[at : at + 8] = core[f, pl.ds(y, 8, stride=8), :]
                    at += 8
            for d, fields in enumerate(FIELDS_Y):
                y = 7 - d if side else d
                for f in fields:
                    out[at : at + 1] = beside_z[f, y : y + 1]
                    at += 1

    by_side("gy", to_one, to_other, send)


def x_kernel(core, beside_z, from_one, from_other, _, beside_y, corner, to_one, to_other):
    lane = iota((8, 128), 1)
    zero = jnp.zeros((8, 128), F32)
    beside_y[...] = jnp.zeros(beside_y.shape, F32)
    corner[...] = jnp.zeros(corner.shape, F32)

    def receive(pairs):
        for source, side in pairs:
            at = 0
            for d, fields in enumerate(FIELDS_Y):
                row = d if side else 7 - d
                for f in fields:
                    into = f ^ 1 if f < 4 else f
                    beside_y[into, pl.ds(row, 8, stride=8), :] = source[at : at + 8]
                    at += 8
            for d, fields in enumerate(FIELDS_Y):
                row = d if side else 7 - d
                for f in fields:
                    into = f ^ 1 if f < 4 else f
                    corner[into, row : row + 1] = source[at : at + 1]
                    at += 1

    by_side("gy", from_one, from_other, receive)

    def send(pairs):
        for out, side in pairs:
            at = 0
            for d, fields in enumerate(FIELDS_X):
                x = 7 - d if side else d
                for f in fields:
                    out[at : at + 8] = core[f, 8 * x : 8 * x + 8]
                    at += 8
            for d, row, f in ROWS_XY:
                from_row = 8 * (7 - d if side else d) + row
                out[at : at + 1] = beside_y[f, from_row : from_row + 1]
                at += 1
            out[at : at + 2] = jnp.zeros((2, 128), F32)
            at += 2
            strips = []
            for f in ALL:
                value = jnp.where((lane >= 48) & (lane < 80), roll(corner[f], -48 if side else 48, 1), beside_z[f])
                strips.append(roll(value, 80 * f - 48 * side, 1))
            for v in range(6):
                value = zero
                for f in ALL:
                    start, stop = max(5 * f, 8 * v), min(5 * f + 5, 8 * v + 8)
                    if start < stop:
                        inside = (lane >= 16 * (start - 8 * v)) & (lane < 16 * (stop - 8 * v))
                        value = jnp.where(inside, strips[f], value)
                out[at : at + 8] = value
                at += 8

    by_side("gx", to_one, to_other, send)


def harmonic(first, second):
    total = first + second
    return 2.0 * first * second / jnp.where(total > 0.0, total, 1.0)


def unpacked(value, slot):
    lane = iota((8, 128), 1)
    value = roll(value, -16 * slot, 1)
    return jnp.where(lane < 3, value, jnp.where(lane >= 117, roll(value, 112, 1), 0.0))


class Planes:
    def __init__(self, inner, outer, first):
        self.inner, self.outer, self.first, self.last = inner, outer, first, 13 - first

    def at(self, p, shift=0):
        if self.first <= p <= self.last - shift:
            return self.inner, p - self.first
        return self.outer, p


def read(planes, p, f=None, tall=16, shift=0):
    ref, p = planes.at(p, shift)
    if isinstance(ref, tuple):
        halves = [half[p] if f is None else half[f, p] for half in ref[: tall // 8]]
        return halves[0] if tall == 8 else jnp.concatenate(halves, axis=0)
    return ref[p, 0:tall] if f is None else ref[f, p, 0:tall]


def write(planes, value, p, f=None, shift=0):
    ref, p = planes.at(p, shift)
    rows = value.shape[0]
    if f is None:
        ref[p, 0:rows] = value
    else:
        ref[f, p, 0:rows] = value


class Block:
    def __init__(self, inner, outer, tops):
        inner = list(inner[:11])
        for i, top in zip((0, 1, 2, 4, 6), tops):
            inner[i] = (top, inner[i])
        names = ("ext", "face_x", "near_x", "face_y", "face_z", "near_y", "near_z", "rest", "weight", "once", "twice")
        first = (3, 3, 3, 3, 3, 3, 3, 3, 4, 4, 5)
        for i, name in enumerate(names):
            setattr(self, name, Planes(inner[i], outer[i] if outer else None, first[i]))
        self.row, self.column = iota((16, 256), 0), iota((16, 256), 1)

    def cells(self, f, p, tall=16):
        return read(self.ext, p, f, tall)

    def side_x(self, planes, p, tall=16):
        return read(planes, p, None, tall, 1)

    def faces_x(self, planes):
        for p in planes:
            face = harmonic(self.cells(PX, p), self.cells(PX, p + 1))
            write(self.face_x, face, p, None, 1)
            write(self.near_x, jnp.where(self.cells(LAYER, p) == self.cells(LAYER, p + 1), face, 0.0), p, None, 1)

    def faces(self, planes):
        for p in planes:
            ids = self.cells(LAYER, p)
            total = self.cells(STORAGE, p)
            for f, axis, face_at, near_at in ((PY, 0, self.face_y, self.near_y), (PZ, 1, self.face_z, self.near_z)):
                across = self.cells(f, p)
                face = harmonic(across, roll(across, -1, axis))
                write(face_at, face, p)
                write(near_at, jnp.where(ids == roll(ids, -1, axis), face, 0.0), p)
                total = total + (face + roll(face, 1, axis))
            write(self.rest, total, p)

    def inner_faces(self, planes):
        for p in planes:
            total = self.cells(STORAGE, p)
            ids, across = self.cells(LAYER, p), self.cells(PY, p)
            face = harmonic(across, roll(across, -1, 0))
            write(self.face_y, face, p)
            write(self.near_y, jnp.where(ids == roll(ids, -1, 0), face, 0.0), p)
            total = total + (face + roll(face, 1, 0))
            face = read(self.face_z, p)
            write(self.rest, total + (face + roll(face, 1, 1)), p)

    def diagonal(self, p):
        return read(self.rest, p) + (self.side_x(self.face_x, p - 1) + self.side_x(self.face_x, p))

    def weights(self, planes):
        for p in planes:
            total = self.diagonal(p)
            write(self.weight, 2.0 / jnp.where(total > 0.0, total, 1.0), p)

    def height(self, p, source):
        return 8 if p in ((1, 12) if source is self.ext else (2, 11)) else 16

    def beside(self, p, source, low=True, high=True):
        tall = self.height(p, source)
        near_y, near_z = read(self.near_y, p), read(self.near_z, p, None, tall)
        near_y_other = jnp.where(self.row == 3, 0.0, near_y)
        totals = []
        for f in range(4):
            whole = read(source, p, f)
            own = whole[0:tall]
            side = near_y_other if f & 1 else near_y
            total = side[0:tall] * roll(whole, -1, 0)[0:tall] + roll(side * whole, 1, 0)[0:tall]
            totals.append(total + (near_z * roll(own, -1, 1) + roll(near_z * own, 1, 1)))
        return self.beside_x(p, source, totals, low, high)

    def beside_x(self, p, source, totals, low=False, high=False):
        tall = self.height(p, source)
        totals = list(totals)
        if low:
            face = self.side_x(self.near_x, p - 1, tall)
            for f in range(2 if p == 7 else 4):
                totals[f] = totals[f] + face * read(source, p - 1, f, tall)
        if high:
            face = self.side_x(self.near_x, p, tall)
            for f in range(2 if p == 6 else 4):
                totals[f] = totals[f] + face * read(source, p + 1, f, tall)
        return totals

    def relax(self, p, source, target, totals):
        gx, gy = lax.axis_index("gx"), lax.axis_index("gy")
        nx, ny = lax.axis_size("gx"), lax.axis_size("gy")
        tall = self.height(p, source)
        row = self.row[0:tall]
        y_valid = jnp.where((row < 4) | (row >= 12), (gy > 0).astype(F32), (gy < ny - 1).astype(F32))
        x_valid = ((gx > 0) if p < 7 else (gx < nx - 1)).astype(F32)
        scale = read(self.weight, p, None, tall)
        scale_other = scale * y_valid
        updated = []
        for f in range(4):
            factor = scale_other if f & 1 else scale
            if f & 2:
                factor = factor * x_valid
            updated.append(read(source, p, f, tall) + factor * totals[f])
        total = (updated[0] + updated[1]) + (updated[2] + updated[3])
        inverse = 1.0 / jnp.where(total > 0.0, total, 1.0)
        for f in range(4):
            write(target, updated[f] * inverse, p, f)

    def sweep(self, planes, source, target):
        for p in planes:
            self.relax(p, source, target, self.beside(p, source))

    def coarse_parts(self, planes, parts):
        row = self.row
        octet = self.octets()
        above, below = (row < 7) | (row == 15), (row > 0) & (row < 9)
        for p in planes:
            inside = 3 <= p <= 10
            ids = self.cells(LAYER, p)
            up, own, down = (jnp.zeros((8, 256), F32) for _ in range(3))
            given = []
            if p >= 4:
                given.append((self.side_x(self.face_x, p - 1, 8), self.side_x(self.near_x, p - 1, 8), self.cells(LAYER, p - 1, 8)))
            if p <= 9:
                given.append((self.side_x(self.face_x, p, 8), self.side_x(self.near_x, p, 8), self.cells(LAYER, p + 1, 8)))
            if inside:
                own = read(self.rest, p, None, 8)
                for face, _, _ in given:
                    own = own + face
                face, near, top = read(self.face_z, p, None, 8), read(self.near_z, p, None, 8), ids[0:8]
                given.append((face, near, roll(top, -1, 1)))
                given.append((roll(face, 1, 1), roll(near, 1, 1), roll(top, 1, 1)))
            for face, near, beside in given:
                apart = face - near
                higher = jnp.where(beside > ids[0:8], apart, 0.0)
                up, own, down = up - higher, own - near, down - (apart - higher)
            total = [up, own, down]
            if inside:
                up, own, down = (jnp.zeros((16, 256), F32) for _ in range(3))
                face, near = read(self.face_y, p), read(self.near_y, p)
                for shift, keep in ((0, above), (1, below)):
                    apart, close = face - near, near
                    beside = roll(ids, 1 if shift else -1, 0)
                    if shift:
                        apart, close = roll(apart, 1, 0), roll(close, 1, 0)
                    apart, close = jnp.where(keep, apart, 0.0), jnp.where(keep, close, 0.0)
                    higher = jnp.where(beside > ids, apart, 0.0)
                    up, own, down = up - higher, own - close, down - (apart - higher)
                total = [jnp.concatenate([t + y[0:8], y[8:16]], axis=0) for t, y in zip(total, (up, own, down))]
            tall = 16 if inside else 8
            lifted = ids[0:tall] > octet[0:tall]
            for oz in range(3):
                upper = jnp.where(lifted, total[oz], 0.0)
                ref, at = parts.at(p)
                ref[oz, 0, at, 0:tall] = total[oz] - upper
                ref[oz, 1, at, 0:tall] = upper

    def coarse_outer_face(self, p, face, parts, outer_parts):
        face = jnp.where(self.row < 8, self.side_x(self.face_x, face), 0.0)
        upper = jnp.where(self.cells(LAYER, p) > self.octets(), face, 0.0)
        ref, at = parts.at(p)
        outer_parts[1, 0, p] = ref[1, 0, at] + (face - upper)
        outer_parts[1, 1, p] = ref[1, 1, at] + upper

    def octets(self):
        octet = (jnp.where(self.column < 192, self.column, self.column - 256) + 256) // BLOCK - 32
        return (octet + lax.axis_index("gz") * (128 // BLOCK)).astype(F32)

    def coarse_sums(self, planes, parts, sums, changed=None, before=None):
        for oz in range(3):
            for lift in range(2):
                for f in range(4):
                    groups = (planes,) if f < 2 else ([p for p in planes if p < 7], [p for p in planes if p >= 7])
                    for i, group in enumerate(groups):
                        if not group:
                            continue
                        top = bottom = None
                        for p in group:
                            part, spot = parts.at(p)
                            if changed is not None and oz == 1 and p in (3, 10):
                                part, spot = changed, p
                            value = part[oz, lift, spot, 0:8] * read(self.twice, p, f, 8)
                            top = value if top is None else top + value
                            if 3 <= p <= 10:
                                ref, at = self.twice.at(p)
                                value = part[oz, lift, spot, 8:16] * ref[f, at, 8:16]
                                bottom = value if bottom is None else bottom + value
                        ox = 1 if f < 2 else 2 * i
                        total = top + (roll(bottom, 4, 0) if f & 1 else bottom)
                        if before is not None:
                            total = total + before[oz, lift, ox, f & 1]
                        sums[oz, lift, ox, f & 1] = total


def store_slots(block, planes, smoothed):
    gx, gy = lax.axis_index("gx"), lax.axis_index("gy")
    rx_own, rx_low, rx_high = gx % 3, (gx + 2) % 3, (gx + 1) % 3
    ry_own, ry_low, ry_high = gy % 3, (gy + 2) % 3, (gy + 1) % 3
    sub = iota((8, 128), 0)
    zero = jnp.zeros((8, 128), F32)
    for i, x in enumerate(planes):
        ids = block.cells(LAYER, x + 3, 8)[:, 0:128]
        residue = ids - 3.0 * jnp.floor((ids + 0.5) * (1.0 / 3.0))
        rx_other, rx_none = (rx_low, rx_high) if x < 4 else (rx_high, rx_low)
        for ex, rx in ((0, rx_own), (1, rx_other)):
            own = read(block.twice, x + 3, 2 * ex, 8)[:, 0:128]
            other = read(block.twice, x + 3, 2 * ex + 1, 8)[:, 0:128]
            low = jnp.where(sub < 4, other, 0.0)
            high = other - low
            for rz in range(3):
                hit = jnp.abs(residue - rz) < 0.5
                smoothed[9 * rz + 3 * ry_own + rx, i] = jnp.where(hit, own, 0.0)
                smoothed[9 * rz + 3 * ry_low + rx, i] = jnp.where(hit, low, 0.0)
                smoothed[9 * rz + 3 * ry_high + rx, i] = jnp.where(hit, high, 0.0)
        for rz in range(3):
            for ry in range(3):
                smoothed[9 * rz + 3 * ry + rx_none, i] = zero


def half_faces(ext, face_x, near_x, face_z, near_z):
    for p in range(8):
        ids = ext[LAYER, p]
        if p < 7:
            face = harmonic(ext[PX, p], ext[PX, p + 1])
            face_x[p] = face
            near_x[p] = jnp.where(ids == ext[LAYER, p + 1], face, 0.0)
        across = ext[PZ, p]
        face = harmonic(across, roll(across, -1, 1))
        face_z[p] = face
        near_z[p] = jnp.where(ids == roll(ids, -1, 1), face, 0.0)


def early_kernel(core, beside_z, ext, *faces):
    for f in ALL:
        for x in range(8):
            ext[f, x, :, 0:128] = core[f, 8 * x : 8 * x + 8]
            ext[f, x, :, 128:256] = unpacked(beside_z[f], x)
    half_faces(ext, *faces)


def inner_kernel(beside_y, corner, *refs):
    tops, arrays, (sums, parts_ref, held_once, held_twice, smoothed_hbm) = refs[:5], refs[5:16], refs[16:21]
    smoothed, sem = refs[21:]
    ext = arrays[0]
    for f in ALL:
        for x in range(8):
            ext[f, x, :, 0:128] = beside_y[f, 8 * x : 8 * x + 8]
            ext[f, x, :, 128:256] = unpacked(corner[f], x)
    half_faces(ext, arrays[1], arrays[2], arrays[4], arrays[6])
    block = Block(arrays, None, tops)
    parts = Planes(parts_ref, None, 3)
    block.inner_faces(range(3, 11))
    block.weights(range(4, 10))
    block.sweep(range(4, 10), block.ext, block.once)
    block.sweep(range(5, 9), block.once, block.twice)
    store_slots(block, (2, 3, 4, 5), smoothed)
    copy = pltpu.make_async_copy(smoothed, smoothed_hbm.at[:, 2:6], sem)
    copy.start()
    for held, source, first, last in ((held_once, block.ext, 3, 10), (held_twice, block.once, 4, 9)):
        for i, p in enumerate((first, last)):
            for f, total in enumerate(block.beside(p, source, low=i == 1, high=i == 0)):
                held[f, i] = total
    block.coarse_parts(range(3, 11), parts)
    block.coarse_sums(list(range(5, 9)), parts, sums)
    copy.wait()


def receive_planes(source, side, ext):
    lane = iota((8, 128), 1)
    zero = jnp.zeros((8, 128), F32)
    planes = (11, 12, 13) if side else (2, 1, 0)
    at = 0
    for d in range(3):
        for f in ALL:
            into = f ^ 2 if f < 4 else f
            if f in FIELDS_X[d]:
                ext[into, planes[d], 0:8, 0:128] = source[at : at + 8]
                at += 8
            else:
                ext[into, planes[d], 0:8, 0:128] = zero
            ext[into, planes[d], 8:16, 0:128] = zero
    for d, row, f in ROWS_XY:
        into = f ^ 2 if f < 4 else f
        ext[into, planes[d], 8 + row : 9 + row, 0:128] = source[at : at + 1]
        at += 1
    at += 2
    for f in ALL:
        into = f ^ 2 if f < 4 else f
        first, last = 5 * f // 8, (5 * f + 4) // 8
        value = source[at + 8 * first : at + 8 * first + 8]
        if last > first:
            value = jnp.where(lane >= 16 * (5 * f % 8), value, source[at + 8 * last : at + 8 * last + 8])
        value = roll(value, 48 * (1 - side) - 80 * f, 1)
        lateral = roll(value, -48 if side else 48, 1)
        for d in range(3):
            slot = d if side else 7 - d
            ext[into, planes[d], 0:8, 128:256] = unpacked(value, slot)
            ext[into, planes[d], 8:16, 128:256] = unpacked(lateral, slot) if d < 2 else zero


def outer_kernel(last, source, *refs):
    tops, arrays, (inner_sums, inner_parts, held_once, held_twice, _), refs = refs[:5], refs[5:16], refs[16:21], refs[21:]
    if last:
        (first_sums, smoothed_hbm, coarse), refs = refs[:3], refs[3:]
    else:
        (smoothed_hbm, sums), refs = refs[:2], refs[2:]
    outer, refs = refs[:11], refs[11:]
    outer_parts, smoothed, sem = refs[:3]
    if last:
        sums = refs[3]
    block = Block(arrays, outer, tops)
    parts = Planes(inner_parts, outer_parts, 3)
    even = lax.axis_index("gx") % 2 == 0
    high = even if last else jnp.logical_not(even)
    copy = pltpu.make_async_copy(smoothed, smoothed_hbm.at[:, pl.ds(jnp.where(high, 6, 0), 2)], sem)
    before = first_sums if last else inner_sums

    def add(side):
        def plane(d):
            return 10 + d if side else 3 - d

        def face(d):
            return 9 + d if side else 3 - d

        receive_planes(source, side, outer[0])
        block.faces_x([face(d) for d in (1, 2, 3)])
        block.faces([plane(1), plane(2)])
        block.weights([plane(0), plane(1), plane(2)])
        steps = (
            (held_once, block.ext, block.once, (2, 1), 0),
            (held_twice, block.once, block.twice, (1, 0), -1),
        )
        for held, values, target, whole, begun in steps:
            block.sweep([plane(d) for d in whole], values, target)
            p = plane(begun)
            totals = [held[f, side] for f in range(4)]
            totals = block.beside_x(p, values, totals, low=not side, high=bool(side))
            block.relax(p, values, target, totals)
        store_slots(block, (6, 7) if side else (0, 1), smoothed)
        copy.start()
        block.coarse_parts([plane(1)], parts)
        block.coarse_outer_face(plane(0), face(1), parts, outer_parts)
        block.coarse_sums(sorted(plane(d) for d in (-1, 0, 1)), parts, sums, outer_parts, before)
        for oz in range(3):
            for lift in range(2):
                ox = 0 if side else 2
                sums[oz, lift, ox] = before[oz, lift, ox]

    pl.when(high)(lambda: add(1))
    pl.when(jnp.logical_not(high))(lambda: add(0))
    if last:
        spot = iota((16, 256), 1)
        place = (jnp.where(spot < 192, spot, spot - 256) + 256) // BLOCK - 32
        row = iota((8, 256), 0)
        for oz in range(3):
            total = jnp.zeros((16, 16), F32)
            for lift in range(2):
                first = second = jnp.zeros((8, 256), F32)
                for ox in range(3):
                    sides = sums[oz, lift, ox, 1]
                    sides = sides + roll(sides, 1, 0)
                    sides = sides + roll(sides, 2, 0)
                    middle = sums[oz, lift, ox, 0]
                    middle = middle + roll(middle, 4, 0)
                    middle = middle + roll(middle, 2, 0)
                    middle = middle + roll(middle, 1, 0)
                    first = jnp.where(row == ox, roll(sides, ox - 3, 0), first)
                    first = jnp.where(row == 3 + ox, middle, first)
                    high = roll(sides, 6 + ox - 7, 0)
                    if ox < 2:
                        first = jnp.where(row == 6 + ox, high, first)
                    else:
                        second = jnp.where(row == 0, high, second)
                chosen = (place + lift - (oz - 1) == iota((16, 256), 0)).astype(F32)
                total = total + lax.dot_general(
                    chosen,
                    jnp.concatenate([first, second], axis=0),
                    (((1,), (1,)), ((), ())),
                    precision=lax.Precision.HIGHEST,
                    preferred_element_type=F32,
                )
            coarse[:, 9 * oz : 9 * oz + 9] = total[:, 0:9] * (1.0 / (BLOCK * BLOCK))
    copy.wait()


VMEM = pl.BlockSpec(memory_space=pltpu.VMEM)
HBM = pl.BlockSpec(memory_space=pltpu.HBM)


def call(kernel, outs, *operands, in_specs=None, out_specs=None, scratch=(), aliases=None, vmem=48 * 1024 * 1024):
    return pl.pallas_call(
        kernel,
        out_shape=[jax.ShapeDtypeStruct(shape, F32) for shape in outs],
        in_specs=in_specs or [VMEM] * len(operands),
        out_specs=out_specs or [VMEM] * len(outs),
        scratch_shapes=scratch,
        input_output_aliases=aliases or {},
        compiler_params=pltpu.CompilerParams(vmem_limit_bytes=vmem),
    )(*operands)


def exchange(axis, to_one, to_other):
    count = lax.axis_size(axis)
    one = [(i, ((i + 1) ^ 1) - 1) for i in range(1, count - 1)]
    other = [(i, i ^ 1) for i in range(count)]
    return lax.ppermute(to_one, axis, one), lax.ppermute(to_other, axis, other)


def per_device(basis, perm, storage, layer):
    block = (FIELDS, 64, 128)
    side = (FIELDS, 8, 128)
    core, edge = call(
        pack_kernel,
        (block, side),
        basis.reshape(27, 64, 128),
        perm.reshape(3, 64, 128),
        storage.reshape(64, 128),
        layer.reshape(64, 128),
        in_specs=[HBM] * 4,
        out_specs=[HBM, HBM],
        vmem=None,
        scratch=[
            pltpu.VMEM(block, F32),
            pltpu.VMEM(side, F32),
            pltpu.VMEM((27, 64, 128), F32),
            pltpu.VMEM((64, 128), jnp.int32),
            pltpu.SemaphoreType.DMA((7,)),
        ],
    )
    other, one = exchange("gz", edge, edge)
    (core,) = call(load_kernel, (block,), core)
    rows = (ROWS_Y + ROWS_Y // 8, 128)
    beside_z, to_one, to_other = call(y_kernel, (side, rows, rows), core, one, other)
    one, other = exchange("gy", to_one, to_other)
    faces = [(7, 8, 256), (7, 8, 256), (8, 8, 256), (8, 8, 256)]
    tops = call(early_kernel, [(FIELDS, 8, 8, 256)] + faces, core, beside_z)
    rows = (ROWS_X + 96, 128)
    beside_y, corner, to_one, to_other = call(x_kernel, (block, side, rows, rows), core, beside_z, one, other, tops[4])
    one, other = exchange("gx", to_one, to_other)

    def arrays(planes):
        return [
            (FIELDS, planes(3), 16, 256),
            (planes(3), 16, 256),
            (planes(3), 16, 256),
            (planes(3), 16, 256),
            (planes(3), 16, 256),
            (planes(3), 16, 256),
            (planes(3), 16, 256),
            (planes(3), 16, 256),
            (planes(4), 16, 256),
            (4, planes(4), 16, 256),
            (4, planes(5), 16, 256),
        ]

    sums = (3, 2, 3, 2, 8, 256)
    whole = (27, 8, 8, 128)
    half = pltpu.VMEM((27, 4, 8, 128), F32)
    held = (4, 2, 16, 256)
    halves = arrays(lambda first: 14 - 2 * first)
    for i, shape in zip((0, 1, 2, 4, 6), [(FIELDS, 8, 8, 256)] + faces):
        halves[i] = shape
    outs = halves + [sums, (3, 2, 8, 16, 256), held, held, whole]
    inner = call(
        inner_kernel,
        outs,
        beside_y,
        corner,
        *tops,
        out_specs=[VMEM] * 15 + [HBM],
        scratch=[half, pltpu.SemaphoreType.DMA],
    )
    scratch = [pltpu.VMEM(shape, F32) for shape in arrays(lambda first: 14)]
    scratch += [pltpu.VMEM((3, 2, 14, 16, 256), F32), pltpu.VMEM((27, 2, 8, 128), F32), pltpu.SemaphoreType.DMA]
    smoothed, first_sums = call(
        functools.partial(outer_kernel, False),
        (whole, sums),
        one,
        *tops,
        *inner,
        in_specs=[VMEM] * 21 + [HBM],
        out_specs=[HBM, VMEM],
        scratch=scratch,
        aliases={21: 0},
    )
    smoothed, coarse = call(
        functools.partial(outer_kernel, True),
        (whole, (16, 27)),
        other,
        *tops,
        *inner[:-1],
        smoothed,
        first_sums,
        in_specs=[VMEM] * 21 + [HBM, VMEM],
        out_specs=[HBM, VMEM],
        scratch=scratch + [pltpu.VMEM(sums, F32)],
        aliases={21: 0},
    )
    return smoothed, coarse.T.reshape(27, 1, 1, 16)


def solution(mesh):
    return jax.shard_map(
        per_device,
        mesh=mesh,
        in_specs=(
            P(None, "gx", "gy", "gz"),
            P(None, "gx", "gy", "gz"),
            P("gx", "gy", "gz"),
            P("gx", "gy", "gz"),
        ),
        out_specs=(P(None, "gx", "gy", "gz"), P(None, "gx", "gy", "gz")),
        check_vma=False,
    )
```

```python
import functools

import jax
import jax.numpy as jnp
from jax import lax
from jax.experimental import pallas as pl
from jax.experimental.pallas import tpu as pltpu
from jax.sharding import PartitionSpec as P

BLOCK = 8
FIELDS = 9
PX, PY, PZ, STORAGE, LAYER = 4, 5, 6, 7, 8
ALL = tuple(range(FIELDS))
FIELDS_X = (ALL, ALL, (0, 1, 2, 3, PX, LAYER))
FIELDS_Y = (ALL, ALL, (0, 1, 2, 3, PY, LAYER))
ROWS_Y = 8 * sum(len(f) for f in FIELDS_Y)
ROWS_X = 8 * sum(len(f) for f in FIELDS_X)
FIELDS_XY = (0, 1, 2, 3, PX, PY, LAYER)
ROWS_XY = (
    [(0, row, f) for row in (7, 0) for f in ALL]
    + [(0, row, f) for row in (6, 1) for f in FIELDS_XY]
    + [(1, row, f) for row in (7, 0) for f in FIELDS_XY]
)
STRIPS = [(2 if f in (PY, PZ, STORAGE) else 3, 1 if f in (PZ, STORAGE) else 2) for f in ALL]
STARTS = [sum(planes + corners for planes, corners in STRIPS[:f]) for f in range(FIELDS + 1)]
F32 = jnp.float32


def iota(shape, dim):
    return lax.broadcasted_iota(jnp.int32, shape, dim)


def roll(value, shift, axis):
    return pltpu.roll(value, shift % value.shape[axis], axis)


def pack_kernel(basis_hbm, perm_hbm, storage_hbm, layer_hbm, core_hbm, edge_hbm, core, edge, basis, layer, sems):
    rest = [
        pltpu.make_async_copy(layer_hbm, layer, sems.at[0]),
        pltpu.make_async_copy(perm_hbm, core.at[PX : PZ + 1], sems.at[1]),
        pltpu.make_async_copy(storage_hbm, core.at[STORAGE], sems.at[2]),
    ]
    arriving = pltpu.make_async_copy(basis_hbm, basis, sems.at[3])
    for copy in rest + [arriving]:
        copy.start()
    gx, gy = lax.axis_index("gx"), lax.axis_index("gy")
    nx, ny = lax.axis_size("gx"), lax.axis_size("gy")
    sub, lane = iota((8, 128), 0), iota((8, 128), 1)
    rx_own, rx_low, rx_high = gx % 3, (gx + 2) % 3, (gx + 1) % 3
    ry_own, ry_low, ry_high = gy % 3, (gy + 2) % 3, (gy + 1) % 3
    low_rows = sub < 4
    y_valid = jnp.where(low_rows, (gy > 0).astype(F32), (gy < ny - 1).astype(F32))

    def moved(value, x):
        return roll(jnp.where(lane < 4, value, roll(value, 16, 1)), 16 * x, 1)

    for copy in rest:
        copy.wait()
    ids = layer[...].astype(F32)
    core[LAYER] = ids
    kept = [pltpu.make_async_copy(core.at[4:9], core_hbm.at[4:9], sems.at[4])]
    kept[0].start()
    residue = ids - 3.0 * jnp.floor((ids + 0.5) * (1.0 / 3.0))
    strip = lane // 16
    for f in range(4, FIELDS):
        packed = jnp.zeros((8, 128), F32)
        for x in range(8):
            packed = jnp.where(strip == x, moved(core[f, 8 * x : 8 * x + 8], x), packed)
        edge[f] = packed

    packed = [jnp.zeros((8, 128), F32) for _ in range(4)]
    arriving.wait()
    for x in range(8):
        here = residue[8 * x : 8 * x + 8]
        is_zero, is_one = here < 0.5, here < 1.5

        def at(rx, ry):
            first, second, third = (basis[9 * rz + 3 * ry + rx, 8 * x : 8 * x + 8] for rz in range(3))
            return jnp.where(is_zero, first, jnp.where(is_one, second, third))

        rx_other = rx_low if x < 4 else rx_high
        x_valid = ((gx > 0) if x < 4 else (gx < nx - 1)).astype(F32)
        for ex, rx in enumerate((rx_own, rx_other)):
            own = at(rx, ry_own)
            other = jnp.where(low_rows, at(rx, ry_low), at(rx, ry_high)) * y_valid
            if ex:
                own, other = own * x_valid, other * x_valid
            for f, value in ((2 * ex, own), (2 * ex + 1, other)):
                core[f, 8 * x : 8 * x + 8] = value
                packed[f] = jnp.where(strip == x, moved(value, x), packed[f])
    for f in range(4):
        edge[f] = packed[f]
    kept.append(pltpu.make_async_copy(edge, edge_hbm, sems.at[5]))
    kept.append(pltpu.make_async_copy(core.at[0:4], core_hbm.at[0:4], sems.at[6]))
    kept[1].start()
    kept[2].start()
    for copy in kept:
        copy.wait()


def load_kernel(core_hbm, core):
    core[...] = core_hbm[...]


def by_side(axis, one, other, body):
    even = lax.axis_index(axis) % 2 == 0
    pl.when(even)(lambda: body(((one, 0), (other, 1))))
    pl.when(jnp.logical_not(even))(lambda: body(((one, 1), (other, 0))))


def y_kernel(core, from_one, from_other, beside_z, to_one, to_other):
    lane = iota((8, 128), 1)
    high = (lane % 16 < 4).astype(jnp.int32)
    odd = lax.axis_index("gz") % 2
    for f in ALL:
        beside_z[f] = jnp.where(high != odd, from_one[f], from_other[f])

    def send(pairs):
        for out, side in pairs:
            at = 0
            for d, fields in enumerate(FIELDS_Y):
                y = 7 - d if side else d
                for f in fields:
                    out[at : at + 8] = core[f, pl.ds(y, 8, stride=8), :]
                    at += 8
            for d, fields in enumerate(FIELDS_Y):
                y = 7 - d if side else d
                for f in fields:
                    out[at : at + 1] = beside_z[f, y : y + 1]
                    at += 1

    by_side("gy", to_one, to_other, send)


def x_kernel(core, beside_z, from_one, from_other, _, beside_y, corner, to_one, to_other):
    lane = iota((8, 128), 1)
    zero = jnp.zeros((8, 128), F32)
    beside_y[...] = jnp.zeros(beside_y.shape, F32)
    corner[...] = jnp.zeros(corner.shape, F32)

    def receive(pairs):
        for source, side in pairs:
            at = 0
            for d, fields in enumerate(FIELDS_Y):
                row = d if side else 7 - d
                for f in fields:
                    into = f ^ 1 if f < 4 else f
                    beside_y[into, pl.ds(row, 8, stride=8), :] = source[at : at + 8]
                    at += 8
            for d, fields in enumerate(FIELDS_Y):
                row = d if side else 7 - d
                for f in fields:
                    into = f ^ 1 if f < 4 else f
                    corner[into, row : row + 1] = source[at : at + 1]
                    at += 1

    by_side("gy", from_one, from_other, receive)

    def send(pairs):
        for out, side in pairs:
            at = 0
            for d, fields in enumerate(FIELDS_X):
                x = 7 - d if side else d
                for f in fields:
                    out[at : at + 8] = core[f, 8 * x : 8 * x + 8]
                    at += 8
            for d, row, f in ROWS_XY:
                from_row = 8 * (7 - d if side else d) + row
                out[at : at + 1] = beside_y[f, from_row : from_row + 1]
                at += 1
            out[at : at + 2] = jnp.zeros((2, 128), F32)
            at += 2
            strips = []
            for f in ALL:
                planes, corners = STRIPS[f]
                if side:
                    start, stop, turn = 128 - 16 * (planes + corners), 128 - 16 * planes, -16 * planes
                else:
                    start, stop, turn = 16 * planes, 16 * (planes + corners), 16 * planes
                value = jnp.where((lane >= start) & (lane < stop), roll(corner[f], turn, 1), beside_z[f])
                strips.append(roll(value, 16 * STARTS[f + side], 1))
            for v in range(STARTS[-1] // 8):
                value = zero
                for f in ALL:
                    start, stop = max(STARTS[f], 8 * v), min(STARTS[f + 1], 8 * v + 8)
                    if start < stop:
                        inside = (lane >= 16 * (start - 8 * v)) & (lane < 16 * (stop - 8 * v))
                        value = jnp.where(inside, strips[f], value)
                out[at : at + 8] = value
                at += 8

    by_side("gx", to_one, to_other, send)


def harmonic(first, second):
    total = first + second
    return 2.0 * first * second / jnp.where(total > 0.0, total, 1.0)


def unpacked(value, slot):
    lane = iota((8, 128), 1)
    value = roll(value, -16 * slot, 1)
    return jnp.where(lane < 3, value, jnp.where(lane >= 117, roll(value, 112, 1), 0.0))


class Planes:
    def __init__(self, inner, outer, first):
        self.inner, self.outer, self.first, self.last = inner, outer, first, 13 - first

    def at(self, p, shift=0):
        if self.first <= p <= self.last - shift:
            return self.inner, p - self.first
        return self.outer, p


def read(planes, p, f=None, tall=16, shift=0):
    ref, p = planes.at(p, shift)
    if isinstance(ref, tuple):
        halves = [half[p] if f is None else half[f, p] for half in ref[: tall // 8]]
        return halves[0] if tall == 8 else jnp.concatenate(halves, axis=0)
    return ref[p, 0:tall] if f is None else ref[f, p, 0:tall]


def write(planes, value, p, f=None, shift=0):
    ref, p = planes.at(p, shift)
    rows = value.shape[0]
    if f is None:
        ref[p, 0:rows] = value
    else:
        ref[f, p, 0:rows] = value


class Block:
    def __init__(self, inner, outer, tops):
        inner = list(inner[:11])
        for i, top in zip((0, 1, 2, 4, 6), tops):
            inner[i] = (top, inner[i])
        names = ("ext", "face_x", "near_x", "face_y", "face_z", "near_y", "near_z", "rest", "weight", "once", "twice")
        first = (3, 3, 3, 3, 3, 3, 3, 3, 4, 4, 5)
        for i, name in enumerate(names):
            setattr(self, name, Planes(inner[i], outer[i] if outer else None, first[i]))
        self.row, self.column = iota((16, 256), 0), iota((16, 256), 1)

    def cells(self, f, p, tall=16):
        return read(self.ext, p, f, tall)

    def side_x(self, planes, p, tall=16):
        return read(planes, p, None, tall, 1)

    def faces_x(self, planes):
        for p in planes:
            face = harmonic(self.cells(PX, p), self.cells(PX, p + 1))
            write(self.face_x, face, p, None, 1)
            write(self.near_x, jnp.where(self.cells(LAYER, p) == self.cells(LAYER, p + 1), face, 0.0), p, None, 1)

    def faces(self, planes):
        for p in planes:
            ids = self.cells(LAYER, p)
            total = self.cells(STORAGE, p)
            for f, axis, face_at, near_at in ((PY, 0, self.face_y, self.near_y), (PZ, 1, self.face_z, self.near_z)):
                across = self.cells(f, p)
                face = harmonic(across, roll(across, -1, axis))
                write(face_at, face, p)
                write(near_at, jnp.where(ids == roll(ids, -1, axis), face, 0.0), p)
                total = total + (face + roll(face, 1, axis))
            write(self.rest, total, p)

    def inner_faces(self, planes):
        for p in planes:
            total = self.cells(STORAGE, p)
            ids, across = self.cells(LAYER, p), self.cells(PY, p)
            face = harmonic(across, roll(across, -1, 0))
            write(self.face_y, face, p)
            write(self.near_y, jnp.where(ids == roll(ids, -1, 0), face, 0.0), p)
            total = total + (face + roll(face, 1, 0))
            face = read(self.face_z, p)
            write(self.rest, total + (face + roll(face, 1, 1)), p)

    def diagonal(self, p):
        return read(self.rest, p) + (self.side_x(self.face_x, p - 1) + self.side_x(self.face_x, p))

    def weights(self, planes):
        for p in planes:
            total = self.diagonal(p)
            write(self.weight, 2.0 / jnp.where(total > 0.0, total, 1.0), p)

    def height(self, p, source):
        return 8 if p in ((1, 12) if source is self.ext else (2, 11)) else 16

    def beside(self, p, source, low=True, high=True):
        tall = self.height(p, source)
        near_y, near_z = read(self.near_y, p), read(self.near_z, p, None, tall)
        near_y_other = jnp.where(self.row == 3, 0.0, near_y)
        totals = []
        for f in range(4):
            whole = read(source, p, f)
            own = whole[0:tall]
            side = near_y_other if f & 1 else near_y
            total = side[0:tall] * roll(whole, -1, 0)[0:tall] + roll(side * whole, 1, 0)[0:tall]
            totals.append(total + (near_z * roll(own, -1, 1) + roll(near_z * own, 1, 1)))
        return self.beside_x(p, source, totals, low, high)

    def beside_x(self, p, source, totals, low=False, high=False):
        tall = self.height(p, source)
        totals = list(totals)
        if low:
            face = self.side_x(self.near_x, p - 1, tall)
            for f in range(2 if p == 7 else 4):
                totals[f] = totals[f] + face * read(source, p - 1, f, tall)
        if high:
            face = self.side_x(self.near_x, p, tall)
            for f in range(2 if p == 6 else 4):
                totals[f] = totals[f] + face * read(source, p + 1, f, tall)
        return totals

    def relax(self, p, source, target, totals):
        gx, gy = lax.axis_index("gx"), lax.axis_index("gy")
        nx, ny = lax.axis_size("gx"), lax.axis_size("gy")
        tall = self.height(p, source)
        row = self.row[0:tall]
        y_valid = jnp.where((row < 4) | (row >= 12), (gy > 0).astype(F32), (gy < ny - 1).astype(F32))
        x_valid = ((gx > 0) if p < 7 else (gx < nx - 1)).astype(F32)
        scale = read(self.weight, p, None, tall)
        scale_other = scale * y_valid
        updated = []
        for f in range(4):
            factor = scale_other if f & 1 else scale
            if f & 2:
                factor = factor * x_valid
            updated.append(read(source, p, f, tall) + factor * totals[f])
        total = (updated[0] + updated[1]) + (updated[2] + updated[3])
        inverse = 1.0 / jnp.where(total > 0.0, total, 1.0)
        for f in range(4):
            write(target, updated[f] * inverse, p, f)

    def sweep(self, planes, source, target):
        for p in planes:
            self.relax(p, source, target, self.beside(p, source))

    def coarse_parts(self, planes, parts):
        row = self.row
        octet = self.octets()
        above, below = (row < 7) | (row == 15), (row > 0) & (row < 9)
        for p in planes:
            inside = 3 <= p <= 10
            ids = self.cells(LAYER, p)
            up, own, down = (jnp.zeros((8, 256), F32) for _ in range(3))
            given = []
            if p >= 4:
                given.append((self.side_x(self.face_x, p - 1, 8), self.side_x(self.near_x, p - 1, 8), self.cells(LAYER, p - 1, 8)))
            if p <= 9:
                given.append((self.side_x(self.face_x, p, 8), self.side_x(self.near_x, p, 8), self.cells(LAYER, p + 1, 8)))
            if inside:
                own = read(self.rest, p, None, 8)
                for face, _, _ in given:
                    own = own + face
                face, near, top = read(self.face_z, p, None, 8), read(self.near_z, p, None, 8), ids[0:8]
                given.append((face, near, roll(top, -1, 1)))
                given.append((roll(face, 1, 1), roll(near, 1, 1), roll(top, 1, 1)))
            for face, near, beside in given:
                apart = face - near
                higher = jnp.where(beside > ids[0:8], apart, 0.0)
                up, own, down = up - higher, own - near, down - (apart - higher)
            total = [up, own, down]
            if inside:
                up, own, down = (jnp.zeros((16, 256), F32) for _ in range(3))
                face, near = read(self.face_y, p), read(self.near_y, p)
                for shift, keep in ((0, above), (1, below)):
                    apart, close = face - near, near
                    beside = roll(ids, 1 if shift else -1, 0)
                    if shift:
                        apart, close = roll(apart, 1, 0), roll(close, 1, 0)
                    apart, close = jnp.where(keep, apart, 0.0), jnp.where(keep, close, 0.0)
                    higher = jnp.where(beside > ids, apart, 0.0)
                    up, own, down = up - higher, own - close, down - (apart - higher)
                total = [jnp.concatenate([t + y[0:8], y[8:16]], axis=0) for t, y in zip(total, (up, own, down))]
            tall = 16 if inside else 8
            lifted = ids[0:tall] > octet[0:tall]
            for oz in range(3):
                upper = jnp.where(lifted, total[oz], 0.0)
                ref, at = parts.at(p)
                ref[oz, 0, at, 0:tall] = total[oz] - upper
                ref[oz, 1, at, 0:tall] = upper

    def coarse_outer_face(self, p, face, parts, outer_parts):
        face = jnp.where(self.row < 8, self.side_x(self.face_x, face), 0.0)
        upper = jnp.where(self.cells(LAYER, p) > self.octets(), face, 0.0)
        ref, at = parts.at(p)
        outer_parts[1, 0, p] = ref[1, 0, at] + (face - upper)
        outer_parts[1, 1, p] = ref[1, 1, at] + upper

    def octets(self):
        octet = (jnp.where(self.column < 192, self.column, self.column - 256) + 256) // BLOCK - 32
        return (octet + lax.axis_index("gz") * (128 // BLOCK)).astype(F32)

    def coarse_sums(self, planes, parts, sums, changed=None, before=None):
        for oz in range(3):
            for lift in range(2):
                for f in range(4):
                    groups = (planes,) if f < 2 else ([p for p in planes if p < 7], [p for p in planes if p >= 7])
                    for i, group in enumerate(groups):
                        if not group:
                            continue
                        top = bottom = None
                        for p in group:
                            part, spot = parts.at(p)
                            if changed is not None and oz == 1 and p in (3, 10):
                                part, spot = changed, p
                            value = part[oz, lift, spot, 0:8] * read(self.twice, p, f, 8)
                            top = value if top is None else top + value
                            if 3 <= p <= 10:
                                ref, at = self.twice.at(p)
                                value = part[oz, lift, spot, 8:16] * ref[f, at, 8:16]
                                bottom = value if bottom is None else bottom + value
                        ox = 1 if f < 2 else 2 * i
                        total = top + (roll(bottom, 4, 0) if f & 1 else bottom)
                        if before is not None:
                            total = total + before[oz, lift, ox, f & 1]
                        sums[oz, lift, ox, f & 1] = total


def store_slots(block, planes, smoothed):
    gx, gy = lax.axis_index("gx"), lax.axis_index("gy")
    rx_own, rx_low, rx_high = gx % 3, (gx + 2) % 3, (gx + 1) % 3
    ry_own, ry_low, ry_high = gy % 3, (gy + 2) % 3, (gy + 1) % 3
    sub = iota((8, 128), 0)
    zero = jnp.zeros((8, 128), F32)
    for i, x in enumerate(planes):
        ids = block.cells(LAYER, x + 3, 8)[:, 0:128]
        residue = ids - 3.0 * jnp.floor((ids + 0.5) * (1.0 / 3.0))
        rx_other, rx_none = (rx_low, rx_high) if x < 4 else (rx_high, rx_low)
        for ex, rx in ((0, rx_own), (1, rx_other)):
            own = read(block.twice, x + 3, 2 * ex, 8)[:, 0:128]
            other = read(block.twice, x + 3, 2 * ex + 1, 8)[:, 0:128]
            low = jnp.where(sub < 4, other, 0.0)
            high = other - low
            for rz in range(3):
                hit = jnp.abs(residue - rz) < 0.5
                smoothed[9 * rz + 3 * ry_own + rx, i] = jnp.where(hit, own, 0.0)
                smoothed[9 * rz + 3 * ry_low + rx, i] = jnp.where(hit, low, 0.0)
                smoothed[9 * rz + 3 * ry_high + rx, i] = jnp.where(hit, high, 0.0)
        for rz in range(3):
            for ry in range(3):
                smoothed[9 * rz + 3 * ry + rx_none, i] = zero


def half_faces(ext, face_x, near_x, face_z, near_z):
    for p in range(8):
        ids = ext[LAYER, p]
        if p < 7:
            face = harmonic(ext[PX, p], ext[PX, p + 1])
            face_x[p] = face
            near_x[p] = jnp.where(ids == ext[LAYER, p + 1], face, 0.0)
        across = ext[PZ, p]
        face = harmonic(across, roll(across, -1, 1))
        face_z[p] = face
        near_z[p] = jnp.where(ids == roll(ids, -1, 1), face, 0.0)


def early_kernel(core, beside_z, ext, *faces):
    for f in ALL:
        for x in range(8):
            ext[f, x, :, 0:128] = core[f, 8 * x : 8 * x + 8]
            ext[f, x, :, 128:256] = unpacked(beside_z[f], x)
    half_faces(ext, *faces)


def inner_kernel(beside_y, corner, *refs):
    tops, arrays, (sums, parts_ref, held_once, held_twice, smoothed_hbm) = refs[:5], refs[5:16], refs[16:21]
    smoothed, sem = refs[21:]
    ext = arrays[0]
    for f in ALL:
        for x in range(8):
            ext[f, x, :, 0:128] = beside_y[f, 8 * x : 8 * x + 8]
            ext[f, x, :, 128:256] = unpacked(corner[f], x)
    half_faces(ext, arrays[1], arrays[2], arrays[4], arrays[6])
    block = Block(arrays, None, tops)
    parts = Planes(parts_ref, None, 3)
    block.inner_faces(range(3, 11))
    block.weights(range(4, 10))
    block.sweep(range(4, 10), block.ext, block.once)
    block.sweep(range(5, 9), block.once, block.twice)
    store_slots(block, (2, 3, 4, 5), smoothed)
    copy = pltpu.make_async_copy(smoothed, smoothed_hbm.at[:, 2:6], sem)
    copy.start()
    for held, source, first, last in ((held_once, block.ext, 3, 10), (held_twice, block.once, 4, 9)):
        for i, p in enumerate((first, last)):
            for f, total in enumerate(block.beside(p, source, low=i == 1, high=i == 0)):
                held[f, i] = total
    block.coarse_parts(range(3, 11), parts)
    block.coarse_sums(list(range(5, 9)), parts, sums)
    copy.wait()


def receive_planes(source, side, ext):
    lane = iota((8, 128), 1)
    zero = jnp.zeros((8, 128), F32)
    planes = (11, 12, 13) if side else (2, 1, 0)
    at = 0
    for d in range(3):
        for f in ALL:
            into = f ^ 2 if f < 4 else f
            if f in FIELDS_X[d]:
                ext[into, planes[d], 0:8, 0:128] = source[at : at + 8]
                at += 8
            else:
                ext[into, planes[d], 0:8, 0:128] = zero
            ext[into, planes[d], 8:16, 0:128] = zero
    for d, row, f in ROWS_XY:
        into = f ^ 2 if f < 4 else f
        ext[into, planes[d], 8 + row : 9 + row, 0:128] = source[at : at + 1]
        at += 1
    at += 2
    for f in ALL:
        into = f ^ 2 if f < 4 else f
        count, corners = STRIPS[f]
        first, last = STARTS[f] // 8, (STARTS[f + 1] - 1) // 8
        value = source[at + 8 * first : at + 8 * first + 8]
        if last > first:
            value = jnp.where(lane >= 16 * (STARTS[f] % 8), value, source[at + 8 * last : at + 8 * last + 8])
        value = roll(value, -16 * STARTS[f if side else f + 1], 1)
        lateral = roll(value, -16 * count if side else 16 * count, 1)
        for d in range(3):
            slot = d if side else 7 - d
            ext[into, planes[d], 0:8, 128:256] = unpacked(value, slot) if d < count else zero
            ext[into, planes[d], 8:16, 128:256] = unpacked(lateral, slot) if d < corners else zero


def outer_kernel(last, source, *refs):
    tops, arrays, (inner_sums, inner_parts, held_once, held_twice, _), refs = refs[:5], refs[5:16], refs[16:21], refs[21:]
    if last:
        (first_sums, smoothed_hbm, coarse), refs = refs[:3], refs[3:]
    else:
        (smoothed_hbm, sums), refs = refs[:2], refs[2:]
    outer, refs = refs[:11], refs[11:]
    outer_parts, smoothed, sem = refs[:3]
    if last:
        sums = refs[3]
    block = Block(arrays, outer, tops)
    parts = Planes(inner_parts, outer_parts, 3)
    even = lax.axis_index("gx") % 2 == 0
    high = even if last else jnp.logical_not(even)
    copy = pltpu.make_async_copy(smoothed, smoothed_hbm.at[:, pl.ds(jnp.where(high, 6, 0), 2)], sem)
    before = first_sums if last else inner_sums

    def add(side):
        def plane(d):
            return 10 + d if side else 3 - d

        def face(d):
            return 9 + d if side else 3 - d

        receive_planes(source, side, outer[0])
        block.faces_x([face(d) for d in (1, 2, 3)])
        block.faces([plane(1), plane(2)])
        block.weights([plane(0), plane(1), plane(2)])
        steps = (
            (held_once, block.ext, block.once, (2, 1), 0),
            (held_twice, block.once, block.twice, (1, 0), -1),
        )
        for held, values, target, whole, begun in steps:
            block.sweep([plane(d) for d in whole], values, target)
            p = plane(begun)
            totals = [held[f, side] for f in range(4)]
            totals = block.beside_x(p, values, totals, low=not side, high=bool(side))
            block.relax(p, values, target, totals)
        store_slots(block, (6, 7) if side else (0, 1), smoothed)
        copy.start()
        block.coarse_parts([plane(1)], parts)
        block.coarse_outer_face(plane(0), face(1), parts, outer_parts)
        block.coarse_sums(sorted(plane(d) for d in (-1, 0, 1)), parts, sums, outer_parts, before)
        for oz in range(3):
            for lift in range(2):
                ox = 0 if side else 2
                sums[oz, lift, ox] = before[oz, lift, ox]

    pl.when(high)(lambda: add(1))
    pl.when(jnp.logical_not(high))(lambda: add(0))
    if last:
        spot = iota((16, 256), 1)
        place = (jnp.where(spot < 192, spot, spot - 256) + 256) // BLOCK - 32
        row = iota((8, 256), 0)
        for oz in range(3):
            total = jnp.zeros((16, 16), F32)
            for lift in range(2):
                first = second = jnp.zeros((8, 256), F32)
                for ox in range(3):
                    sides = sums[oz, lift, ox, 1]
                    sides = sides + roll(sides, 1, 0)
                    sides = sides + roll(sides, 2, 0)
                    middle = sums[oz, lift, ox, 0]
                    middle = middle + roll(middle, 4, 0)
                    middle = middle + roll(middle, 2, 0)
                    middle = middle + roll(middle, 1, 0)
                    first = jnp.where(row == ox, roll(sides, ox - 3, 0), first)
                    first = jnp.where(row == 3 + ox, middle, first)
                    high = roll(sides, 6 + ox - 7, 0)
                    if ox < 2:
                        first = jnp.where(row == 6 + ox, high, first)
                    else:
                        second = jnp.where(row == 0, high, second)
                chosen = (place + lift - (oz - 1) == iota((16, 256), 0)).astype(F32)
                total = total + lax.dot_general(
                    chosen,
                    jnp.concatenate([first, second], axis=0),
                    (((1,), (1,)), ((), ())),
                    precision=lax.Precision.HIGHEST,
                    preferred_element_type=F32,
                )
            coarse[:, 9 * oz : 9 * oz + 9] = total[:, 0:9] * (1.0 / (BLOCK * BLOCK))
    copy.wait()


VMEM = pl.BlockSpec(memory_space=pltpu.VMEM)
HBM = pl.BlockSpec(memory_space=pltpu.HBM)


def call(kernel, outs, *operands, in_specs=None, out_specs=None, scratch=(), aliases=None, vmem=48 * 1024 * 1024):
    return pl.pallas_call(
        kernel,
        out_shape=[jax.ShapeDtypeStruct(shape, F32) for shape in outs],
        in_specs=in_specs or [VMEM] * len(operands),
        out_specs=out_specs or [VMEM] * len(outs),
        scratch_shapes=scratch,
        input_output_aliases=aliases or {},
        compiler_params=pltpu.CompilerParams(vmem_limit_bytes=vmem),
    )(*operands)


def exchange(axis, to_one, to_other):
    count = lax.axis_size(axis)
    one = [(i, ((i + 1) ^ 1) - 1) for i in range(1, count - 1)]
    other = [(i, i ^ 1) for i in range(count)]
    return lax.ppermute(to_one, axis, one), lax.ppermute(to_other, axis, other)


def per_device(basis, perm, storage, layer):
    block = (FIELDS, 64, 128)
    side = (FIELDS, 8, 128)
    core, edge = call(
        pack_kernel,
        (block, side),
        basis.reshape(27, 64, 128),
        perm.reshape(3, 64, 128),
        storage.reshape(64, 128),
        layer.reshape(64, 128),
        in_specs=[HBM] * 4,
        out_specs=[HBM, HBM],
        vmem=None,
        scratch=[
            pltpu.VMEM(block, F32),
            pltpu.VMEM(side, F32),
            pltpu.VMEM((27, 64, 128), F32),
            pltpu.VMEM((64, 128), jnp.int32),
            pltpu.SemaphoreType.DMA((7,)),
        ],
    )
    other, one = exchange("gz", edge, edge)
    (core,) = call(load_kernel, (block,), core)
    rows = (ROWS_Y + ROWS_Y // 8, 128)
    beside_z, to_one, to_other = call(y_kernel, (side, rows, rows), core, one, other)
    one, other = exchange("gy", to_one, to_other)
    faces = [(7, 8, 256), (7, 8, 256), (8, 8, 256), (8, 8, 256)]
    tops = call(early_kernel, [(FIELDS, 8, 8, 256)] + faces, core, beside_z)
    rows = (ROWS_X + 48 + STARTS[-1], 128)
    beside_y, corner, to_one, to_other = call(x_kernel, (block, side, rows, rows), core, beside_z, one, other, tops[4])
    one, other = exchange("gx", to_one, to_other)

    def arrays(planes):
        return [
            (FIELDS, planes(3), 16, 256),
            (planes(3), 16, 256),
            (planes(3), 16, 256),
            (planes(3), 16, 256),
            (planes(3), 16, 256),
            (planes(3), 16, 256),
            (planes(3), 16, 256),
            (planes(3), 16, 256),
            (planes(4), 16, 256),
            (4, planes(4), 16, 256),
            (4, planes(5), 16, 256),
        ]

    sums = (3, 2, 3, 2, 8, 256)
    whole = (27, 8, 8, 128)
    half = pltpu.VMEM((27, 4, 8, 128), F32)
    held = (4, 2, 16, 256)
    halves = arrays(lambda first: 14 - 2 * first)
    for i, shape in zip((0, 1, 2, 4, 6), [(FIELDS, 8, 8, 256)] + faces):
        halves[i] = shape
    outs = halves + [sums, (3, 2, 8, 16, 256), held, held, whole]
    inner = call(
        inner_kernel,
        outs,
        beside_y,
        corner,
        *tops,
        out_specs=[VMEM] * 15 + [HBM],
        scratch=[half, pltpu.SemaphoreType.DMA],
    )
    scratch = [pltpu.VMEM(shape, F32) for shape in arrays(lambda first: 14)]
    scratch += [pltpu.VMEM((3, 2, 14, 16, 256), F32), pltpu.VMEM((27, 2, 8, 128), F32), pltpu.SemaphoreType.DMA]
    smoothed, first_sums = call(
        functools.partial(outer_kernel, False),
        (whole, sums),
        one,
        *tops,
        *inner,
        in_specs=[VMEM] * 21 + [HBM],
        out_specs=[HBM, VMEM],
        scratch=scratch,
        aliases={21: 0},
    )
    smoothed, coarse = call(
        functools.partial(outer_kernel, True),
        (whole, (16, 27)),
        other,
        *tops,
        *inner[:-1],
        smoothed,
        first_sums,
        in_specs=[VMEM] * 21 + [HBM, VMEM],
        out_specs=[HBM, VMEM],
        scratch=scratch + [pltpu.VMEM(sums, F32)],
        aliases={21: 0},
    )
    return smoothed, coarse.T.reshape(27, 1, 1, 16)


def solution(mesh):
    return jax.shard_map(
        per_device,
        mesh=mesh,
        in_specs=(
            P(None, "gx", "gy", "gz"),
            P(None, "gx", "gy", "gz"),
            P("gx", "gy", "gz"),
            P("gx", "gy", "gz"),
        ),
        out_specs=(P(None, "gx", "gy", "gz"), P(None, "gx", "gy", "gz")),
        check_vma=False,
    )
```
